32 devices in a mesh: head: 2 (over x), blk: 16 (over z, y, core).
Axes of the slice: x: 2, y: 2, z: 4, core: 2. Of those that a mesh axis runs over, the one named last changes fastest.
Arguments:
- query_rows: bfloat16 [512, 1536], P(('head', 'blk')), may hold values from -400 to 400
- key_rows: bfloat16 [512, 1536], P(('head', 'blk')), may hold values from -400 to 400
- value_rows: bfloat16 [512, 1536], P(('head', 'blk')), may hold values from -6 to 6
- residual: bfloat16 [512, 1536], P(('head', 'blk')), may hold values from -6 to 6
- out_weight: bfloat16 [1536, 1536], P('head'), may hold values from -0.15625 to 0.15625
- attention_gate: float32 [1536], replicated, may hold values from 0.5 to 1.5
- norm_shift: float32 [1536], replicated, may hold values from -1 to 1
- norm_scale: float32 [1536], replicated, may hold values from -0.5 to 0.5
- expert_gate: float32 [1536], replicated, may hold values from 0.5 to 1.5
- expert_up: bfloat16 [16, 1536, 4096], P('blk', None, 'head'), may hold values from -0.15625 to 0.15625
- expert_down: bfloat16 [16, 4096, 1536], P('blk', 'head'), may hold values from -0.09375 to 0.09375
- routing: int32 [512, 2], P(('head', 'blk')), may hold values from 0 to 15, as said below
- combine_weight: float32 [512, 2], P(('head', 'blk')), may hold values from 0.2 to 1
Outputs:
- mixed: bfloat16 [512, 1536], P(('head', 'blk'))
The draws below stay inside these ranges and needn't reach their ends.
Inputs may be any that keep to these rules, and one draw needn't show every extreme that they name: `routing`: the two choices of a token differ. Within the 16 tokens of one device every expert is named at most 2 times, and one expert, the same for every device, is named exactly 2 times by every device.
All inputs are finite; a program needn't handle non-finite values.
Results may differ from the reference program's by a relative error of at most 0.011.
Values may be sent and summed in bfloat16 or wider, within the bound.
A program may use at most 64 MiB of HBM per device.

```python
import math
import jax
import jax.numpy as jnp
from jax import lax

D = 1536
HEADS = 24
HD = 64
FF = 4096
TOPK = 2
TOK_DEV = 16
CAP = 2
TOKENS = 512
EXPERTS = 16
N_HEAD = 2
N_BLK = 16


def draw_query_rows(key, part):
    base = jnp.clip(jax.random.normal(jax.random.fold_in(key, 1), (TOKENS, D)) * 2.5, -15.0, 15.0)
    return base.astype(jnp.bfloat16)


def draw_key_rows(key, part):
    base = jnp.clip(jax.random.normal(jax.random.fold_in(key, 2), (TOKENS, D)), -6.0, 6.0)
    return base.astype(jnp.bfloat16)


def draw_routing(key, part):
    hot_expert = jax.random.randint(jax.random.fold_in(key, 31), (), 0, EXPERTS).astype(jnp.int32)
    block_total = TOKENS // TOK_DEV
    keys_perm = jax.random.split(jax.random.fold_in(key, 32), block_total)
    keys_order = jax.random.split(jax.random.fold_in(key, 33), block_total)
    keys_side = jax.random.split(jax.random.fold_in(key, 34), block_total)

    def one_block(key_perm, key_order, key_side):
        shuffled = jax.random.permutation(key_perm, EXPERTS - 1).astype(jnp.int32)
        others = shuffled + (shuffled >= hot_expert).astype(jnp.int32)
        repeated = jnp.tile(others, CAP)
        sequence = jnp.concatenate([jnp.full((CAP,), hot_expert, jnp.int32), repeated])[:TOPK * TOK_DEV]
        first_choice = sequence[:TOK_DEV]
        second_choice = sequence[TOK_DEV:TOPK * TOK_DEV]
        swapped = jax.random.randint(key_side, (TOK_DEV,), 0, 2)
        left_side = jnp.where(swapped == 1, second_choice, first_choice)
        right_side = jnp.where(swapped == 1, first_choice, second_choice)
        paired = jnp.stack([left_side, right_side], axis=1)
        row_order = jax.random.permutation(key_order, TOK_DEV)
        return paired[row_order]
    return jax.vmap(one_block)(keys_perm, keys_order, keys_side).reshape(TOKENS, TOPK).astype(jnp.int32)


def steps_of(key, dims, cuts, smallest, top_value):
    level = 1.0
    for dim, blocks in cuts:
        draws = jax.random.uniform(jax.random.fold_in(jax.random.fold_in(key, 6), dim), (blocks,), jnp.float32, smallest / len(cuts), top_value / len(cuts))
        level = level * jnp.repeat(jnp.exp(draws), dims[dim] // blocks).reshape((-1,) + (1,) * (len(dims) - 1 - dim))
    return level


def centred(key, shape, spread, limit, shards=(), kind=jnp.bfloat16):
    array = spread * jax.random.normal(key, shape, jnp.float32)
    if shards:
        array = array * steps_of(key, shape, shards, -0.22, 0.18)
    return jnp.clip(array, -limit, limit).astype(kind)


def setup_inputs(seed: int = 0) -> dict:
    streams_of = jax.random.split(jax.random.key(seed), 14)
    query_rows = draw_query_rows(jax.random.fold_in(streams_of[13], 71), 0)
    key_rows = draw_key_rows(jax.random.fold_in(streams_of[13], 71), 0)
    value_rows = centred(streams_of[2], (TOKENS, D), 1.0, 6.0, ((0, 32),))
    residual = centred(streams_of[3], (TOKENS, D), 1.0, 6.0, ((0, 32),))
    out_weight = centred(streams_of[4], (D, D), D ** -0.5, 0.15625, ((0, 2),))
    attention_gate = jnp.clip(jax.random.uniform(streams_of[5], (D,), jnp.float32, 0.5, 1.5), 0.5, 1.5)
    norm_shift = jnp.clip(jax.random.uniform(streams_of[6], (D,), jnp.float32, -1.0, 1.0), -1.0, 1.0)
    norm_scale = jnp.clip(jax.random.uniform(streams_of[7], (D,), jnp.float32, -0.5, 0.5), -0.5, 0.5)
    expert_gate = jnp.clip(jax.random.uniform(streams_of[8], (D,), jnp.float32, 0.5, 1.5), 0.5, 1.5)
    expert_up = centred(streams_of[9], (EXPERTS, D, FF), D ** -0.5, 0.15625, ((0, 16), (2, 2)))
    expert_down = centred(streams_of[10], (EXPERTS, FF, D), FF ** -0.5, 0.09375, ((0, 16), (1, 2)))
    routing = draw_routing(jax.random.fold_in(streams_of[13], 71), 0)
    combine_weight = jnp.clip(0.2 + 0.8 * jax.random.uniform(streams_of[12], (TOKENS, TOPK), jnp.float32) ** steps_of(streams_of[12], (TOKENS, TOPK), ((0, 32),), -0.2, 0.2), 0.2, 1.0)
    return {"query_rows": query_rows, "key_rows": key_rows, "value_rows": value_rows, "residual": residual, "out_weight": out_weight, "attention_gate": attention_gate, "norm_shift": norm_shift, "norm_scale": norm_scale, "expert_gate": expert_gate, "expert_up": expert_up, "expert_down": expert_down, "routing": routing, "combine_weight": combine_weight}


def one_head(operands):
    query_head, key_head, value_head = operands
    scores = jnp.dot(query_head, key_head.T, preferred_element_type=jnp.float32) * (1.0 / math.sqrt(HD))
    peak = lax.optimization_barrier(jnp.max(scores, axis=1, keepdims=True))
    probs = jnp.exp(scores - peak)
    denom = lax.optimization_barrier(jnp.sum(probs, axis=1, keepdims=True))
    numer = jnp.dot(probs.astype(jnp.bfloat16), value_head, preferred_element_type=jnp.float32)
    return numer / denom

def reference(query_rows, key_rows, value_rows, residual, out_weight, attention_gate, norm_shift, norm_scale, expert_gate, expert_up, expert_down, routing, combine_weight):
    total_rows = query_rows.shape[0]

    def split_heads(matrix):
        return matrix.reshape(total_rows, HEADS, HD).transpose(1, 0, 2)
    per_head = lax.map(one_head, (split_heads(query_rows), split_heads(key_rows), split_heads(value_rows)))
    attended = per_head.transpose(1, 0, 2).reshape(total_rows, D).astype(jnp.bfloat16)
    group_width = D // N_HEAD
    projected = jnp.zeros((total_rows, D), jnp.float32)
    for group in range(N_HEAD):
        part_sum = jnp.dot(attended[:, group * group_width:(group + 1) * group_width], out_weight[group * group_width:(group + 1) * group_width], preferred_element_type=jnp.float32).astype(jnp.bfloat16)
        projected = projected + lax.optimization_barrier(part_sum).astype(jnp.float32)
    middle = residual.astype(jnp.float32) + attention_gate * projected
    average = lax.optimization_barrier(jnp.mean(middle, axis=1, keepdims=True))
    centered = middle - average
    variance = lax.optimization_barrier(jnp.mean(centered * centered, axis=1, keepdims=True))
    normed = (centered * lax.rsqrt(variance + 1e-06) * (1.0 + norm_scale) + norm_shift).astype(jnp.bfloat16)
    entries = routing.reshape(-1).astype(jnp.int32)
    entry_count = entries.shape[0]
    devices_all = N_HEAD * N_BLK
    per_source = entries.reshape(devices_all, TOPK * TOK_DEV)
    onehot = (per_source[:, :, None] == jnp.arange(EXPERTS, dtype=jnp.int32)[None, None, :]).astype(jnp.int32)
    before = jnp.cumsum(onehot, axis=1) - onehot
    slot_number = lax.optimization_barrier(jnp.sum(before * onehot, axis=2)).reshape(-1).astype(jnp.int32)
    source = jnp.arange(entry_count, dtype=jnp.int32) // (TOPK * TOK_DEV)
    position = (source * CAP + slot_number).astype(jnp.int32)
    buffer_rows = devices_all * CAP
    ff_group = FF // N_HEAD

    def one_expert(results, expert):
        chosen = entries == expert
        target = jnp.where(chosen, position, buffer_rows).astype(jnp.int32)
        entry_of_slot = jnp.zeros((buffer_rows,), jnp.int32).at[target].set(jnp.arange(entry_count, dtype=jnp.int32), mode='drop')
        rows_in = normed[entry_of_slot // TOPK]
        hidden = jax.nn.gelu(jnp.dot(rows_in, expert_up[expert], preferred_element_type=jnp.float32), approximate=True).astype(jnp.bfloat16)
        down_here = expert_down[expert]
        summed = jnp.zeros((buffer_rows, D), jnp.float32)
        for group in range(N_HEAD):
            part_sum = jnp.dot(hidden[:, group * ff_group:(group + 1) * ff_group], down_here[group * ff_group:(group + 1) * ff_group], preferred_element_type=jnp.float32).astype(jnp.bfloat16)
            summed = summed + lax.optimization_barrier(part_sum).astype(jnp.float32)
        expert_out = summed.astype(jnp.bfloat16)
        return (jnp.where(chosen[:, None], expert_out[position], results), None)
    results, _ = lax.scan(one_expert, jnp.zeros((entry_count, D), jnp.bfloat16), jnp.arange(EXPERTS, dtype=jnp.int32))
    mixture = lax.optimization_barrier(jnp.sum(results.reshape(total_rows, TOPK, D).astype(jnp.float32) * combine_weight[:, :, None], axis=1))
    return (middle + expert_gate * mixture).astype(jnp.bfloat16)
```

```python
import functools
import math

import jax
import jax.numpy as jnp
from jax import lax
from jax.experimental import pallas as pl
from jax.experimental.pallas import tpu as pltpu
from jax.sharding import PartitionSpec as P

HD = 64
TOPK = 2
LANES = 128
MESH = pl.DeviceIdType.MESH
F32 = jnp.float32
BF16 = jnp.bfloat16


def round_up(value, step):
    return -(-value // step) * step


def dot(left, right):
    return lax.dot_general(left, right, (((1,), (0,)), ((), ())), preferred_element_type=F32)


def dot_nt(left, right):
    return lax.dot_general(left, right, (((1,), (1,)), ((), ())), preferred_element_type=F32)


def dot_tn(left, right):
    return lax.dot_general(left, right, (((0,), (0,)), ((), ())), preferred_element_type=F32)


def wait_bytes(ref, sem):
    pltpu.make_async_copy(ref, ref, sem).wait()


def kernel(
    dims,
    q_ref, k_ref, v_ref, res_ref, ag_ref, shift_ref, scale_ref, eg_ref, route_ref, comb_ref,
    ow_hbm, up_hbm, down_hbm,
    out_ref,
    ow, up, down,
    kvs, kvr, qs, qr, ats, atr, ps, pr, sb, xr, eb, rr,
    mid, wide, thin, hidden, flat,
    wsem, ssem, rsem,
):
    nh, nb, sub, cap = dims
    n = nh * nb
    quarter = nb // sub
    tok, width = q_ref.shape
    gcols = width // (nh * sub)
    heads = gcols // HD
    win = qs.shape[2]
    kvcols = kvs.shape[2]
    klo = kvcols - win
    pieces = width // LANES
    h = lax.axis_index("head")
    b = lax.axis_index("blk")
    me = h * nb + b
    k_own = b // quarter
    m_own = lax.rem(b, quarter)

    fetch = [
        pltpu.make_async_copy(ow_hbm, ow, wsem.at[0]),
        pltpu.make_async_copy(up_hbm.at[0], up, wsem.at[1]),
        pltpu.make_async_copy(down_hbm.at[0], down, wsem.at[2]),
    ]
    for copy in fetch:
        copy.start()

    barrier = pltpu.get_barrier_semaphore()

    def greet(step, carry):
        to = lax.rem(me + step, n)
        pl.semaphore_signal(
            barrier, inc=1, device_id=(to // nb, lax.rem(to, nb)), device_id_type=MESH
        )
        return carry

    lax.fori_loop(1, n, greet, 0)

    for g in range(nh * sub):
        cols = slice(g * gcols, (g + 1) * gcols)
        kvs[g, :, 0:gcols] = v_ref[:, cols]
        kvs[g, :, kvcols - gcols:kvcols] = k_ref[:, cols]
        if kvcols > 2 * gcols:
            kvs[g, :, gcols:kvcols - gcols] = jnp.zeros((tok, kvcols - 2 * gcols), BF16)
        if win > gcols:
            qs[g, :, 0:win - gcols] = jnp.zeros((tok, win - gcols), BF16)
        qs[g, :, win - gcols:win] = q_ref[:, cols]

    pl.semaphore_wait(barrier, n - 1)

    def remote(src, dst, phase, to_h, to_b):
        pltpu.make_async_remote_copy(
            src_ref=src, dst_ref=dst, send_sem=ssem.at[phase], recv_sem=rsem.at[phase],
            device_id=(to_h, to_b), device_id_type=MESH,
        ).start()

    def local(src, dst, phase):
        pltpu.make_async_copy(src, dst, rsem.at[phase]).start()

    def send_q(step, carry):
        group = lax.rem(h * sub + k_own + step, nh * sub)
        to_h, to_s = group // sub, lax.rem(group, sub)
        remote(qs.at[group], qr.at[k_own * nh + h], 1, to_h, to_s * quarter + m_own)
        return carry

    lax.fori_loop(1, nh * sub, send_q, 0)
    local(qs.at[h * sub + k_own], qr.at[k_own * nh + h], 1)

    def send_kv(step, carry):
        to = lax.rem(me + step, n)
        to_h, to_b = to // nb, lax.rem(to, nb)
        remote(kvs.at[to_h * sub + to_b // quarter], kvr.at[me], 0, to_h, to_b)
        return carry

    lax.fori_loop(1, n, send_kv, 0)
    local(kvs.at[h * sub + k_own], kvr.at[me], 0)

    slots = nb * cap
    row = lax.broadcasted_iota(jnp.int32, (slots, tok), 0)
    expert = row // cap
    place = (row - expert * cap).astype(F32)
    first = route_ref[0:1, :] == expert
    second = route_ref[1:2, :] == expert
    named = jnp.where(first | second, 1.0, 0.0)
    tri = jnp.where(
        lax.broadcasted_iota(jnp.int32, (tok, tok), 0) < lax.broadcasted_iota(jnp.int32, (tok, tok), 1),
        1.0, 0.0,
    )
    earlier = dot(named.astype(BF16), tri.astype(BF16))
    here = earlier == place
    pick = [jnp.where(choice & here, 1.0, 0.0) for choice in (first, second)]
    eye = lax.broadcasted_iota(jnp.int32, (tok, tok), 0) == lax.broadcasted_iota(jnp.int32, (tok, tok), 1)

    wait_bytes(qr, rsem.at[1])
    wait_bytes(kvr, rsem.at[0])

    rows = nh * sub * tok
    queries = qr[...].reshape(rows, win)
    keys = kvr[:, :, klo:kvcols].reshape(n * tok, win)
    values = kvr[:, :, 0:win].reshape(n * tok, win)
    lane = lax.broadcasted_iota(jnp.int32, (rows, win), 1)
    attended = jnp.zeros((rows, win), F32)
    for j in range(heads):
        lo = win - gcols + j * HD
        q_j = jnp.where((lane >= lo) & (lane < lo + HD), queries, jnp.zeros_like(queries))
        scores = dot_nt(q_j, keys) * (1.0 / math.sqrt(HD))
        probs = jnp.exp(scores - jnp.max(scores, axis=1, keepdims=True))
        total = jnp.sum(probs, axis=1, keepdims=True)
        numer = dot(probs.astype(BF16), values)
        attended = jnp.where((lane >= j * HD) & (lane < (j + 1) * HD), numer / total, attended)
    ats[...] = attended.astype(BF16).reshape(sub, nh * tok, win)

    def send_att(step, carry):
        to_k = lax.rem(k_own + step, sub)
        remote(ats.at[to_k], atr.at[k_own], 2, h, to_k * quarter + m_own)
        return carry

    lax.fori_loop(1, sub, send_att, 0)
    local(ats.at[k_own], atr.at[k_own], 2)
    fetch[0].wait()
    wait_bytes(atr, rsem.at[2])

    partial = jnp.zeros((nh * tok, width), F32)
    for s in range(sub):
        partial = partial + dot(atr[s, :, 0:gcols], ow[s * gcols:(s + 1) * gcols, :])
    ps[...] = partial.astype(BF16).reshape(nh, tok, width)

    def send_part(step, carry):
        to_h = lax.rem(h + step, nh)
        remote(ps.at[to_h], pr.at[h], 3, to_h, b)
        return carry

    lax.fori_loop(1, nh, send_part, 0)
    local(ps.at[h], pr.at[h], 3)
    wait_bytes(pr, rsem.at[3])

    projected = jnp.sum(pr[...].astype(F32), axis=0)
    middle = res_ref[...].astype(F32) + ag_ref[...] * projected
    average = jnp.mean(middle, axis=1, keepdims=True)
    centered = middle - average
    variance = jnp.mean(centered * centered, axis=1, keepdims=True)
    normed = (
        centered * lax.rsqrt(variance + 1e-06) * (1.0 + scale_ref[...]) + shift_ref[...]
    ).astype(BF16)
    mid[...] = middle

    buffer = dot((pick[0] + pick[1]).astype(BF16), normed)
    for c in range(pieces):
        thin[pl.ds(c, slots, pieces), :] = buffer[:, c * LANES:(c + 1) * LANES]
    sb[...] = thin[...].reshape(sb.shape).astype(BF16)

    def send_rows(step, carry):
        to = lax.rem(me + step, n)
        to_h, to_b = to // nb, lax.rem(to, nb)
        remote(sb.at[to_b], xr.at[me], 4, to_h, to_b)
        return carry

    lax.fori_loop(1, n, send_rows, 0)
    local(sb.at[b], xr.at[me], 4)
    fetch[1].wait()
    wait_bytes(xr, rsem.at[4])

    wide[...] = xr[...].astype(F32).reshape(wide.shape)
    for c in range(pieces):
        flat[:, c * LANES:(c + 1) * LANES] = wide[pl.ds(c, n * cap, pieces), :].astype(BF16)

    ff = up.shape[1]
    up_tile = math.gcd(ff, 512)

    def up_step(i, carry):
        cols = pl.ds(pl.multiple_of(i * up_tile, up_tile), up_tile)
        u = dot(flat[...], up[:, cols])
        inner = math.sqrt(2.0 / math.pi) * (u + 0.044715 * (u * u * u))
        hidden[:, cols] = (0.5 * u * (1.0 + jnp.tanh(inner))).astype(BF16)
        return carry

    lax.fori_loop(0, ff // up_tile, up_step, 0)
    fetch[2].wait()
    down_tile = math.gcd(width, 512)
    for i in range(width // down_tile):
        part = dot(hidden[...], down[:, i * down_tile:(i + 1) * down_tile])
        for c in range(down_tile // LANES):
            wide[pl.ds(i * (down_tile // LANES) + c, n * cap, pieces), :] = part[:, c * LANES:(c + 1) * LANES]
    eb[...] = wide[...].reshape(eb.shape).astype(BF16)

    def send_back(step, carry):
        to = lax.rem(me + step, n)
        remote(eb.at[to], rr.at[me], 5, to // nb, lax.rem(to, nb))
        return carry

    lax.fori_loop(1, n, send_back, 0)
    local(eb.at[me], rr.at[me], 5)

    wait_bytes(kvr.at[pl.ds(0, n - 1)], ssem.at[0])
    wait_bytes(qr.at[pl.ds(0, nh * sub - 1)], ssem.at[1])
    if sub > 1:
        wait_bytes(atr.at[pl.ds(0, sub - 1)], ssem.at[2])
    wait_bytes(pr.at[pl.ds(0, nh - 1)], ssem.at[3])
    wait_bytes(xr.at[pl.ds(0, n - 1)], ssem.at[4])

    wait_bytes(rr, rsem.at[5])
    summed = rr[0:nb].astype(F32)
    for other in range(1, nh):
        summed = summed + rr[other * nb:(other + 1) * nb].astype(F32)
    thin[...] = summed.reshape(thin.shape)
    weights = [
        jnp.sum(jnp.where(eye, comb_ref[i:i + 1, :], 0.0), axis=1, keepdims=True) for i in range(TOPK)
    ]
    back = jnp.concatenate(
        [thin[pl.ds(c, slots, pieces), :].astype(BF16) for c in range(pieces)], axis=1
    )
    mixture = weights[0] * dot_tn(pick[0].astype(BF16), back)
    mixture = mixture + weights[1] * dot_tn(pick[1].astype(BF16), back)
    out_ref[...] = (mid[...] + eg_ref[...] * mixture).astype(BF16)
    wait_bytes(rr.at[pl.ds(0, n - 1)], ssem.at[5])


def on_device(
    nh, nb,
    query_rows, key_rows, value_rows, residual, out_weight, attention_gate, norm_shift, norm_scale,
    expert_gate, expert_up, expert_down, routing, combine_weight,
):
    tok, width = query_rows.shape
    n = nh * nb
    cap = max(2, TOPK * tok // nb)
    sub = math.gcd(width // HD // nh, nb)
    gcols = width // (nh * sub)
    win = round_up(gcols, LANES)
    kvcols = round_up(2 * gcols, LANES)
    pieces = width // LANES
    block = cap * pieces
    ff = expert_up.shape[2]
    vmem = pl.BlockSpec(memory_space=pltpu.VMEM)
    anywhere = pl.BlockSpec(memory_space=pl.ANY)
    as_row = lambda vector: vector.reshape(1, width)
    return pl.pallas_call(
        functools.partial(kernel, (nh, nb, sub, cap)),
        out_shape=jax.ShapeDtypeStruct((tok, width), BF16),
        in_specs=[vmem] * 10 + [anywhere] * 3,
        out_specs=vmem,
        scratch_shapes=[
            pltpu.VMEM(out_weight.shape, BF16),
            pltpu.VMEM(expert_up.shape[1:], BF16),
            pltpu.VMEM(expert_down.shape[1:], BF16),
            pltpu.VMEM((nh * sub, tok, kvcols), BF16),
            pltpu.VMEM((n, tok, kvcols), BF16),
            pltpu.VMEM((nh * sub, tok, win), BF16),
            pltpu.VMEM((nh * sub, tok, win), BF16),
            pltpu.VMEM((sub, nh * tok, win), BF16),
            pltpu.VMEM((sub, nh * tok, win), BF16),
            pltpu.VMEM((nh, tok, width), BF16),
            pltpu.VMEM((nh, tok, width), BF16),
            pltpu.VMEM((nb, block, LANES), BF16),
            pltpu.VMEM((n, block, LANES), BF16),
            pltpu.VMEM((n, block, LANES), BF16),
            pltpu.VMEM((n, block, LANES), BF16),
            pltpu.VMEM((tok, width), F32),
            pltpu.VMEM((n * block, LANES), F32),
            pltpu.VMEM((nb * block, LANES), F32),
            pltpu.VMEM((n * cap, ff), BF16),
            pltpu.VMEM((n * cap, width), BF16),
            pltpu.SemaphoreType.DMA((3,)),
            pltpu.SemaphoreType.DMA((6,)),
            pltpu.SemaphoreType.DMA((6,)),
        ],
        compiler_params=pltpu.CompilerParams(
            collective_id=0, has_side_effects=True, vmem_limit_bytes=60 * 1024 * 1024
        ),
        name="layer",
    )(
        query_rows, key_rows, value_rows, residual,
        as_row(attention_gate), as_row(norm_shift), as_row(norm_scale), as_row(expert_gate),
        routing.T, combine_weight.T,
        out_weight, expert_up, expert_down,
    )


def solution(mesh):
    tokens = P(("head", "blk"), None)
    in_specs = (
        tokens, tokens, tokens, tokens,
        P("head", None), P(), P(), P(), P(),
        P("blk", None, "head"), P("blk", "head", None), tokens, tokens,
    )
    return jax.shard_map(
        functools.partial(on_device, mesh.shape["head"], mesh.shape["blk"]),
        mesh=mesh, in_specs=in_specs, out_specs=tokens, check_vma=False,
    )
```

```python
import functools
import math

import jax
import jax.numpy as jnp
from jax import lax
from jax.experimental import pallas as pl
from jax.experimental.pallas import tpu as pltpu
from jax.sharding import PartitionSpec as P

HD = 64
TOPK = 2
LANES = 128
MESH = pl.DeviceIdType.MESH
F32 = jnp.float32
BF16 = jnp.bfloat16


def round_up(value, step):
    return -(-value // step) * step


def dot(left, right):
    return lax.dot_general(left, right, (((1,), (0,)), ((), ())), preferred_element_type=F32)


def dot_nt(left, right):
    return lax.dot_general(left, right, (((1,), (1,)), ((), ())), preferred_element_type=F32)


def dot_tn(left, right):
    return lax.dot_general(left, right, (((0,), (0,)), ((), ())), preferred_element_type=F32)


def wrap(index, size):
    return jnp.where(index >= size, index - size, index)


def wait_bytes(ref, sem):
    pltpu.make_async_copy(ref, ref, sem).wait()


def kernel(
    dims,
    q_ref, k_ref, v_ref, res_ref, ag_ref, shift_ref, scale_ref, eg_ref, route_ref, comb_ref,
    ow_hbm, up_hbm, down_hbm,
    out_ref,
    ow, up, down,
    kvs, kvr, qs, qr, ats, atr, ps, pr, sb, xr, eb, rr,
    mid, wide, thin, hidden, flat,
    wsem, ssem, rsem,
):
    nh, nb, sub, cap = dims
    n = nh * nb
    quarter = nb // sub
    tok, width = q_ref.shape
    gcols = width // (nh * sub)
    heads = gcols // HD
    win = qs.shape[2]
    kvcols = kvs.shape[2]
    klo = kvcols - win
    pieces = width // LANES
    h = lax.axis_index("head")
    b = lax.axis_index("blk")
    me = h * nb + b
    k_own = lax.div(b, quarter)
    m_own = b - k_own * quarter
    side = lax.rem(b, 2)
    half = n // 2
    half_me = h * (nb // 2) + lax.div(b, 2)

    fetch = [
        pltpu.make_async_copy(ow_hbm, ow, wsem.at[0]),
        pltpu.make_async_copy(up_hbm.at[0], up, wsem.at[1]),
        pltpu.make_async_copy(down_hbm.at[0], down, wsem.at[2]),
    ]
    for copy in fetch:
        copy.start()

    barrier = pltpu.get_barrier_semaphore()

    def each_other(act):
        for far in range(nh):
            to_h = wrap(h + far, nh)

            def step_to(step, carry, to_h=to_h):
                act(to_h, wrap(b + step, nb))
                return carry

            lax.fori_loop(1 if far == 0 else 0, nb, step_to, 0, unroll=nb <= 16)

    def greet(to_h, to_b):
        pl.semaphore_signal(barrier, inc=1, device_id=(to_h, to_b), device_id_type=MESH)

    each_other(greet)

    for g in range(nh * sub):
        cols = slice(g * gcols, (g + 1) * gcols)
        kvs[g, :, 0:gcols] = v_ref[:, cols]
        kvs[g, :, kvcols - gcols:kvcols] = k_ref[:, cols]
        if kvcols > 2 * gcols:
            kvs[g, :, gcols:kvcols - gcols] = jnp.zeros((tok, kvcols - 2 * gcols), BF16)
        if win > gcols:
            qs[g, :, 0:win - gcols] = jnp.zeros((tok, win - gcols), BF16)
        qs[g, :, win - gcols:win] = q_ref[:, cols]

    pl.semaphore_wait(barrier, n - 1)

    def remote(src, dst, phase, to_h, to_b):
        pltpu.make_async_remote_copy(
            src_ref=src, dst_ref=dst, send_sem=ssem.at[phase], recv_sem=rsem.at[phase],
            device_id=(to_h, to_b), device_id_type=MESH,
        ).start()

    def local(src, dst, phase):
        pltpu.make_async_copy(src, dst, rsem.at[phase]).start()

    for far in range(nh):
        to_h = wrap(h + far, nh)
        for step in range(sub):
            to_s = wrap(k_own + step, sub)
            source, target = qs.at[to_h * sub + to_s], qr.at[k_own * nh + h]
            if far == 0 and step == 0:
                local(source, target, 1)
            else:
                remote(source, target, 1, to_h, to_s * quarter + m_own)

    for far in range(nh):
        to_h = wrap(h + far, nh)

        def send_kv(step, carry, to_h=to_h):
            to_b = wrap(b + 2 * step, nb)
            source = kvs.at[to_h * sub + lax.div(to_b, quarter)]
            remote(source, kvr.at[side, half_me], 0, to_h, to_b)
            return carry

        lax.fori_loop(1 if far == 0 else 0, nb // 2, send_kv, 0, unroll=nb <= 16)
    local(kvs.at[h * sub + k_own], kvr.at[side, half_me], 0)

    slots = nb * cap
    row = lax.broadcasted_iota(jnp.int32, (slots, tok), 0)
    expert = row // cap
    place = (row - expert * cap).astype(F32)
    first = route_ref[0:1, :] == expert
    second = route_ref[1:2, :] == expert
    named = jnp.where(first | second, 1.0, 0.0)
    tri = jnp.where(
        lax.broadcasted_iota(jnp.int32, (tok, tok), 0) < lax.broadcasted_iota(jnp.int32, (tok, tok), 1),
        1.0, 0.0,
    )
    earlier = dot(named.astype(BF16), tri.astype(BF16))
    here = earlier == place
    pick = [jnp.where(choice & here, 1.0, 0.0) for choice in (first, second)]
    eye = lax.broadcasted_iota(jnp.int32, (tok, tok), 0) == lax.broadcasted_iota(jnp.int32, (tok, tok), 1)

    wait_bytes(kvr.at[side], rsem.at[0])
    pltpu.make_async_remote_copy(
        src_ref=kvr.at[side], dst_ref=kvr.at[side], send_sem=ssem.at[6], recv_sem=rsem.at[6],
        device_id=(h, b + 1 - 2 * side), device_id_type=MESH,
    ).start()
    wait_bytes(qr, rsem.at[1])

    rows = nh * sub * tok
    queries = qr[...].reshape(rows, win)
    lane = lax.broadcasted_iota(jnp.int32, (rows, win), 1)
    lows = [win - gcols + j * HD for j in range(heads)]
    split_q = [
        jnp.where((lane >= lo) & (lane < lo + HD), queries, jnp.zeros_like(queries)) for lo in lows
    ]

    def score_half(which):
        keys = kvr[which, :, :, klo:kvcols].reshape(half * tok, win)
        return [dot_nt(q_j, keys) * (1.0 / math.sqrt(HD)) for q_j in split_q]

    near_scores = score_half(side)
    near_values = kvr[side, :, :, 0:win].reshape(half * tok, win)
    wait_bytes(kvr.at[1 - side], rsem.at[6])
    far_scores = score_half(1 - side)
    far_values = kvr[1 - side, :, :, 0:win].reshape(half * tok, win)
    attended = jnp.zeros((rows, win), F32)
    for j in range(heads):
        peak = jnp.maximum(
            jnp.max(near_scores[j], axis=1, keepdims=True), jnp.max(far_scores[j], axis=1, keepdims=True)
        )
        near = jnp.exp(near_scores[j] - peak)
        far = jnp.exp(far_scores[j] - peak)
        total = jnp.sum(near, axis=1, keepdims=True) + jnp.sum(far, axis=1, keepdims=True)
        numer = dot(near.astype(BF16), near_values) + dot(far.astype(BF16), far_values)
        attended = jnp.where((lane >= j * HD) & (lane < (j + 1) * HD), numer / total, attended)
    ats[...] = attended.astype(BF16).reshape(sub, nh * tok, win)

    for step in range(1, sub):
        to_k = wrap(k_own + step, sub)
        remote(ats.at[to_k], atr.at[k_own], 2, h, to_k * quarter + m_own)
    local(ats.at[k_own], atr.at[k_own], 2)
    fetch[0].wait()
    wait_bytes(atr, rsem.at[2])

    partial = jnp.zeros((nh * tok, width), F32)
    for s in range(sub):
        partial = partial + dot(atr[s, :, 0:gcols], ow[s * gcols:(s + 1) * gcols, :])
    ps[...] = partial.astype(BF16).reshape(nh, tok, width)

    for far in range(1, nh):
        to_h = wrap(h + far, nh)
        remote(ps.at[to_h], pr.at[h], 3, to_h, b)
    local(ps.at[h], pr.at[h], 3)
    wait_bytes(pr, rsem.at[3])

    projected = jnp.sum(pr[...].astype(F32), axis=0)
    middle = res_ref[...].astype(F32) + ag_ref[...] * projected
    average = jnp.mean(middle, axis=1, keepdims=True)
    centered = middle - average
    variance = jnp.mean(centered * centered, axis=1, keepdims=True)
    normed = (
        centered * lax.rsqrt(variance + 1e-06) * (1.0 + scale_ref[...]) + shift_ref[...]
    ).astype(BF16)
    mid[...] = middle

    buffer = dot((pick[0] + pick[1]).astype(BF16), normed)
    for c in range(pieces):
        thin[pl.ds(c, slots, pieces), :] = buffer[:, c * LANES:(c + 1) * LANES]
    sb[...] = thin[...].reshape(sb.shape).astype(BF16)

    each_other(lambda to_h, to_b: remote(sb.at[to_b], xr.at[me], 4, to_h, to_b))
    local(sb.at[b], xr.at[me], 4)
    fetch[1].wait()
    wait_bytes(xr, rsem.at[4])

    wide[...] = xr[...].astype(F32).reshape(wide.shape)
    for c in range(pieces):
        flat[:, c * LANES:(c + 1) * LANES] = wide[pl.ds(c, n * cap, pieces), :].astype(BF16)

    ff = up.shape[1]
    up_tile = math.gcd(ff, 512)

    def up_step(i, carry):
        cols = pl.ds(pl.multiple_of(i * up_tile, up_tile), up_tile)
        u = dot(flat[...], up[:, cols])
        inner = math.sqrt(2.0 / math.pi) * (u + 0.044715 * (u * u * u))
        hidden[:, cols] = (0.5 * u * (1.0 + jnp.tanh(inner))).astype(BF16)
        return carry

    lax.fori_loop(0, ff // up_tile, up_step, 0)
    fetch[2].wait()
    down_tile = math.gcd(width, 512)
    for i in range(width // down_tile):
        part = dot(hidden[...], down[:, i * down_tile:(i + 1) * down_tile])
        for c in range(down_tile // LANES):
            wide[pl.ds(i * (down_tile // LANES) + c, n * cap, pieces), :] = part[:, c * LANES:(c + 1) * LANES]
    eb[...] = wide[...].reshape(eb.shape).astype(BF16)

    each_other(lambda to_h, to_b: remote(eb.at[to_h * nb + to_b], rr.at[me], 5, to_h, to_b))
    local(eb.at[me], rr.at[me], 5)

    wait_bytes(kvr.at[0, pl.ds(0, half - 1)], ssem.at[0])
    wait_bytes(kvr.at[side], ssem.at[6])
    wait_bytes(qr.at[pl.ds(0, nh * sub - 1)], ssem.at[1])
    if sub > 1:
        wait_bytes(atr.at[pl.ds(0, sub - 1)], ssem.at[2])
    wait_bytes(pr.at[pl.ds(0, nh - 1)], ssem.at[3])
    wait_bytes(xr.at[pl.ds(0, n - 1)], ssem.at[4])

    wait_bytes(rr, rsem.at[5])
    summed = rr[0:nb].astype(F32)
    for other in range(1, nh):
        summed = summed + rr[other * nb:(other + 1) * nb].astype(F32)
    thin[...] = summed.reshape(thin.shape)
    weights = [
        jnp.sum(jnp.where(eye, comb_ref[i:i + 1, :], 0.0), axis=1, keepdims=True) for i in range(TOPK)
    ]
    back = jnp.concatenate(
        [thin[pl.ds(c, slots, pieces), :].astype(BF16) for c in range(pieces)], axis=1
    )
    mixture = weights[0] * dot_tn(pick[0].astype(BF16), back)
    mixture = mixture + weights[1] * dot_tn(pick[1].astype(BF16), back)
    out_ref[...] = (mid[...] + eg_ref[...] * mixture).astype(BF16)
    wait_bytes(rr.at[pl.ds(0, n - 1)], ssem.at[5])


def on_device(
    nh, nb,
    query_rows, key_rows, value_rows, residual, out_weight, attention_gate, norm_shift, norm_scale,
    expert_gate, expert_up, expert_down, routing, combine_weight,
):
    tok, width = query_rows.shape
    n = nh * nb
    cap = max(2, TOPK * tok // nb)
    sub = math.gcd(width // HD // nh, nb)
    gcols = width // (nh * sub)
    win = round_up(gcols, LANES)
    kvcols = round_up(2 * gcols, LANES)
    pieces = width // LANES
    block = cap * pieces
    ff = expert_up.shape[2]
    vmem = pl.BlockSpec(memory_space=pltpu.VMEM)
    anywhere = pl.BlockSpec(memory_space=pl.ANY)
    return pl.pallas_call(
        functools.partial(kernel, (nh, nb, sub, cap)),
        out_shape=jax.ShapeDtypeStruct((tok, width), BF16),
        in_specs=[vmem] * 10 + [anywhere] * 3,
        out_specs=vmem,
        scratch_shapes=[
            pltpu.VMEM(out_weight.shape, BF16),
            pltpu.VMEM(expert_up.shape[1:], BF16),
            pltpu.VMEM(expert_down.shape[1:], BF16),
            pltpu.VMEM((nh * sub, tok, kvcols), BF16),
            pltpu.VMEM((2, n // 2, tok, kvcols), BF16),
            pltpu.VMEM((nh * sub, tok, win), BF16),
            pltpu.VMEM((nh * sub, tok, win), BF16),
            pltpu.VMEM((sub, nh * tok, win), BF16),
            pltpu.VMEM((sub, nh * tok, win), BF16),
            pltpu.VMEM((nh, tok, width), BF16),
            pltpu.VMEM((nh, tok, width), BF16),
            pltpu.VMEM((nb, block, LANES), BF16),
            pltpu.VMEM((n, block, LANES), BF16),
            pltpu.VMEM((n, block, LANES), BF16),
            pltpu.VMEM((n, block, LANES), BF16),
            pltpu.VMEM((tok, width), F32),
            pltpu.VMEM((n * block, LANES), F32),
            pltpu.VMEM((nb * block, LANES), F32),
            pltpu.VMEM((n * cap, ff), BF16),
            pltpu.VMEM((n * cap, width), BF16),
            pltpu.SemaphoreType.DMA((3,)),
            pltpu.SemaphoreType.DMA((7,)),
            pltpu.SemaphoreType.DMA((7,)),
        ],
        compiler_params=pltpu.CompilerParams(
            collective_id=0, has_side_effects=True, vmem_limit_bytes=60 * 1024 * 1024
        ),
        name="layer",
    )(
        query_rows, key_rows, value_rows, residual,
        attention_gate, norm_shift, norm_scale, expert_gate,
        routing.T, combine_weight.T,
        out_weight, expert_up, expert_down,
    )


def solution(mesh):
    tokens = P(("head", "blk"), None)
    in_specs = (
        tokens, tokens, tokens, tokens,
        P("head", None), P(), P(), P(), P(),
        P("blk", None, "head"), P("blk", "head", None), tokens, tokens,
    )
    return jax.shard_map(
        functools.partial(on_device, mesh.shape["head"], mesh.shape["blk"]),
        mesh=mesh, in_specs=in_specs, out_specs=tokens, check_vma=False,
    )
```

```python
import functools
import math

import jax
import jax.numpy as jnp
from jax import lax
from jax.experimental import pallas as pl
from jax.experimental.pallas import tpu as pltpu
from jax.sharding import PartitionSpec as P

HD = 64
TOPK = 2
LANES = 128
MESH = pl.DeviceIdType.MESH
F32 = jnp.float32
BF16 = jnp.bfloat16


def round_up(value, step):
    return -(-value // step) * step


def dot(left, right):
    return lax.dot_general(left, right, (((1,), (0,)), ((), ())), preferred_element_type=F32)


def dot_nt(left, right):
    return lax.dot_general(left, right, (((1,), (1,)), ((), ())), preferred_element_type=F32)


def dot_tn(left, right):
    return lax.dot_general(left, right, (((0,), (0,)), ((), ())), preferred_element_type=F32)


def wrap(index, size):
    return jnp.where(index >= size, index - size, index)


def wait_bytes(ref, sem):
    pltpu.make_async_copy(ref, ref, sem).wait()


def kernel(
    dims,
    q_hbm, k_hbm, v_hbm, res_hbm, ag_hbm, shift_hbm, scale_hbm, eg_hbm, route_hbm, comb_hbm,
    ow_hbm, up_hbm, down_hbm,
    out_ref,
    q_ref, k_ref, v_ref, res_ref, ag_ref, shift_ref, scale_ref, eg_ref, route_ref, comb_ref,
    ow, up, down,
    kvs, kvr, qs, qr, ats, atr, ps, pr, sb, xr, es, er, eb, rr,
    mid, wide, thin, hidden, flat,
    isem, wsem, ssem, rsem, esend, erecv,
):
    nh, nb, sub, cap = dims
    n = nh * nb
    quarter = nb // sub
    tok, width = q_ref.shape
    gcols = width // (nh * sub)
    heads = gcols // HD
    win = qs.shape[2]
    kvcols = kvs.shape[2]
    klo = kvcols - win
    pieces = width // LANES
    h = lax.axis_index("head")
    b = lax.axis_index("blk")
    me = h * nb + b
    k_own = lax.div(b, quarter)
    m_own = b - k_own * quarter
    side = lax.rem(b, 2)
    half = n // 2
    half_me = h * (nb // 2) + lax.div(b, 2)

    inputs = [
        pltpu.make_async_copy(source, target, isem.at[i])
        for i, (source, target) in enumerate((
            (v_hbm, v_ref), (k_hbm, k_ref), (q_hbm, q_ref), (res_hbm, res_ref), (ag_hbm, ag_ref),
            (shift_hbm, shift_ref), (scale_hbm, scale_ref), (eg_hbm, eg_ref), (route_hbm, route_ref),
            (comb_hbm, comb_ref),
        ))
    ]
    for copy in inputs:
        copy.start()
    fetch = [
        pltpu.make_async_copy(ow_hbm, ow, wsem.at[0]),
        pltpu.make_async_copy(up_hbm.at[0], up, wsem.at[1]),
        pltpu.make_async_copy(down_hbm.at[0], down, wsem.at[2]),
    ]
    for copy in fetch:
        copy.start()

    barrier = pltpu.get_barrier_semaphore()

    def each_other(act):
        for far in range(nh):
            to_h = wrap(h + far, nh)

            def step_to(step, carry, to_h=to_h):
                act(to_h, wrap(b + step, nb))
                return carry

            lax.fori_loop(1 if far == 0 else 0, nb, step_to, 0, unroll=nb <= 16)

    def greet(to_h, to_b):
        pl.semaphore_signal(barrier, inc=1, device_id=(to_h, to_b), device_id_type=MESH)

    each_other(greet)

    for copy in inputs:
        copy.wait()

    for g in range(nh * sub):
        cols = slice(g * gcols, (g + 1) * gcols)
        kvs[g, :, 0:gcols] = v_ref[:, cols]
        kvs[g, :, kvcols - gcols:kvcols] = k_ref[:, cols]
        if kvcols > 2 * gcols:
            kvs[g, :, gcols:kvcols - gcols] = jnp.zeros((tok, kvcols - 2 * gcols), BF16)
        if win > gcols:
            qs[g, :, 0:win - gcols] = jnp.zeros((tok, win - gcols), BF16)
        qs[g, :, win - gcols:win] = q_ref[:, cols]

    pl.semaphore_wait(barrier, n - 1)

    def remote(src, dst, phase, to_h, to_b):
        pltpu.make_async_remote_copy(
            src_ref=src, dst_ref=dst, send_sem=ssem.at[phase], recv_sem=rsem.at[phase],
            device_id=(to_h, to_b), device_id_type=MESH,
        ).start()

    def local(src, dst, phase):
        pltpu.make_async_copy(src, dst, rsem.at[phase]).start()

    for far in range(nh):
        to_h = wrap(h + far, nh)
        for step in range(sub):
            to_s = wrap(k_own + step, sub)
            source, target = qs.at[to_h * sub + to_s], qr.at[k_own * nh + h]
            if far == 0 and step == 0:
                local(source, target, 1)
            else:
                remote(source, target, 1, to_h, to_s * quarter + m_own)

    for far in range(nh):
        to_h = wrap(h + far, nh)

        def send_kv(step, carry, to_h=to_h):
            to_b = wrap(b + 2 * step, nb)
            source = kvs.at[to_h * sub + lax.div(to_b, quarter)]
            remote(source, kvr.at[side, half_me], 0, to_h, to_b)
            return carry

        lax.fori_loop(1 if far == 0 else 0, nb // 2, send_kv, 0, unroll=nb <= 16)
    local(kvs.at[h * sub + k_own], kvr.at[side, half_me], 0)

    slots = nb * cap
    row = lax.broadcasted_iota(jnp.int32, (slots, tok), 0)
    expert = row // cap
    place = (row - expert * cap).astype(F32)
    first = route_ref[0:1, :] == expert
    second = route_ref[1:2, :] == expert
    named = jnp.where(first | second, 1.0, 0.0)
    tri = jnp.where(
        lax.broadcasted_iota(jnp.int32, (tok, tok), 0) < lax.broadcasted_iota(jnp.int32, (tok, tok), 1),
        1.0, 0.0,
    )
    earlier = dot(named.astype(BF16), tri.astype(BF16))
    here = earlier == place
    pick = [jnp.where(choice & here, 1.0, 0.0) for choice in (first, second)]
    eye = lax.broadcasted_iota(jnp.int32, (tok, tok), 0) == lax.broadcasted_iota(jnp.int32, (tok, tok), 1)

    wait_bytes(kvr.at[side], rsem.at[0])
    pltpu.make_async_remote_copy(
        src_ref=kvr.at[side], dst_ref=kvr.at[side], send_sem=ssem.at[6], recv_sem=rsem.at[6],
        device_id=(h, b + 1 - 2 * side), device_id_type=MESH,
    ).start()
    wait_bytes(qr, rsem.at[1])

    rows = nh * sub * tok
    queries = qr[...].reshape(rows, win)
    lane = lax.broadcasted_iota(jnp.int32, (rows, win), 1)
    lows = [win - gcols + j * HD for j in range(heads)]
    split_q = jnp.concatenate(
        [jnp.where((lane >= lo) & (lane < lo + HD), queries, jnp.zeros_like(queries)) for lo in lows], axis=0
    )

    def score_half(which):
        keys = kvr[which, :, :, klo:kvcols].reshape(half * tok, win)
        return dot_nt(split_q, keys) * (1.0 / math.sqrt(HD))

    near_scores = score_half(side)
    near_peak = jnp.max(near_scores, axis=1, keepdims=True)
    near_values = kvr[side, :, :, 0:win].reshape(half * tok, win)
    wait_bytes(kvr.at[1 - side], rsem.at[6])
    far_scores = score_half(1 - side)
    far_values = kvr[1 - side, :, :, 0:win].reshape(half * tok, win)
    peak = jnp.maximum(near_peak, jnp.max(far_scores, axis=1, keepdims=True))
    near = jnp.exp(near_scores - peak)
    far = jnp.exp(far_scores - peak)
    total = jnp.sum(near, axis=1, keepdims=True) + jnp.sum(far, axis=1, keepdims=True)
    stacked = (dot(near.astype(BF16), near_values) + dot(far.astype(BF16), far_values)) / total
    attended = jnp.zeros((rows, win), F32)
    for j in range(heads):
        attended = jnp.where(
            (lane >= j * HD) & (lane < (j + 1) * HD), stacked[j * rows:(j + 1) * rows], attended
        )
    ats[...] = attended.astype(BF16).reshape(sub, nh * tok, win)

    for step in range(1, sub):
        to_k = wrap(k_own + step, sub)
        remote(ats.at[to_k], atr.at[k_own], 2, h, to_k * quarter + m_own)
    local(ats.at[k_own], atr.at[k_own], 2)
    fetch[0].wait()
    wait_bytes(atr, rsem.at[2])

    partial = jnp.zeros((nh * tok, width), F32)
    for s in range(sub):
        partial = partial + dot(atr[s, :, 0:gcols], ow[s * gcols:(s + 1) * gcols, :])
    ps[...] = partial.astype(BF16).reshape(nh, tok, width)

    for far in range(1, nh):
        to_h = wrap(h + far, nh)
        remote(ps.at[to_h], pr.at[h], 3, to_h, b)
    local(ps.at[h], pr.at[h], 3)
    wait_bytes(pr, rsem.at[3])

    projected = jnp.sum(pr[...].astype(F32), axis=0)
    middle = res_ref[...].astype(F32) + ag_ref[...] * projected
    average = jnp.mean(middle, axis=1, keepdims=True)
    centered = middle - average
    variance = jnp.mean(centered * centered, axis=1, keepdims=True)
    normed = (
        centered * lax.rsqrt(variance + 1e-06) * (1.0 + scale_ref[...]) + shift_ref[...]
    ).astype(BF16)
    mid[...] = middle

    buffer = dot((pick[0] + pick[1]).astype(BF16), normed)
    for c in range(pieces):
        thin[pl.ds(c, slots, pieces), :] = buffer[:, c * LANES:(c + 1) * LANES]
    sb[...] = thin[...].reshape(sb.shape).astype(BF16)

    each_other(lambda to_h, to_b: remote(sb.at[to_b], xr.at[me], 4, to_h, to_b))
    local(sb.at[b], xr.at[me], 4)
    fetch[1].wait()
    wait_bytes(xr, rsem.at[4])

    wide[...] = xr[...].astype(F32).reshape(wide.shape)
    for c in range(pieces):
        flat[:, c * LANES:(c + 1) * LANES] = wide[pl.ds(c, n * cap, pieces), :].astype(BF16)

    ff = up.shape[1]
    up_tile = math.gcd(ff, 512)

    def up_step(i, carry):
        cols = pl.ds(pl.multiple_of(i * up_tile, up_tile), up_tile)
        u = dot(flat[...], up[:, cols])
        inner = math.sqrt(2.0 / math.pi) * (u + 0.044715 * (u * u * u))
        hidden[:, cols] = (0.5 * u * (1.0 + jnp.tanh(inner))).astype(BF16)
        return carry

    lax.fori_loop(0, ff // up_tile, up_step, 0)
    fetch[2].wait()
    tiles, _, back_rows, down_tile = es.shape
    tile_pieces = down_tile // LANES

    def tile_copy(i, far):
        to_h = wrap(h + far, nh)
        return pltpu.make_async_remote_copy(
            src_ref=es.at[i, to_h], dst_ref=er.at[i, far - 1], send_sem=esend.at[i, far - 1],
            recv_sem=erecv.at[i, far - 1], device_id=(to_h, b), device_id_type=MESH,
        )

    for i in range(tiles):
        part = dot(hidden[...], down[:, i * down_tile:(i + 1) * down_tile])
        es[i] = part.astype(BF16).reshape(nh, back_rows, down_tile)
        for far in range(1, nh):
            tile_copy(i, far).start()
    for i in range(tiles):
        both = es[i, h].astype(F32)
        for far in range(1, nh):
            tile_copy(i, far).wait_recv()
            both = both + er[i, far - 1].astype(F32)
        for c in range(tile_pieces):
            thin[pl.ds(i * tile_pieces + c, slots, pieces), :] = both[:, c * LANES:(c + 1) * LANES]
    eb[...] = thin[...].reshape(eb.shape).astype(BF16)

    def send_back(step, carry):
        to_b = wrap(b + step, nb)
        remote(eb.at[to_b], rr.at[b], 5, h, to_b)
        return carry

    lax.fori_loop(1, nb, send_back, 0, unroll=nb <= 16)
    local(eb.at[b], rr.at[b], 5)

    wait_bytes(kvr.at[0, pl.ds(0, half - 1)], ssem.at[0])
    wait_bytes(kvr.at[side], ssem.at[6])
    wait_bytes(qr.at[pl.ds(0, nh * sub - 1)], ssem.at[1])
    if sub > 1:
        wait_bytes(atr.at[pl.ds(0, sub - 1)], ssem.at[2])
    wait_bytes(pr.at[pl.ds(0, nh - 1)], ssem.at[3])
    wait_bytes(xr.at[pl.ds(0, n - 1)], ssem.at[4])

    wait_bytes(rr, rsem.at[5])
    thin[...] = rr[...].astype(F32).reshape(thin.shape)
    weights = [
        jnp.sum(jnp.where(eye, comb_ref[i:i + 1, :], 0.0), axis=1, keepdims=True) for i in range(TOPK)
    ]
    back = jnp.concatenate(
        [thin[pl.ds(c, slots, pieces), :].astype(BF16) for c in range(pieces)], axis=1
    )
    mixture = weights[0] * dot_tn(pick[0].astype(BF16), back)
    mixture = mixture + weights[1] * dot_tn(pick[1].astype(BF16), back)
    out_ref[...] = (mid[...] + eg_ref[...] * mixture).astype(BF16)
    wait_bytes(rr.at[pl.ds(0, nb - 1)], ssem.at[5])
    for i in range(tiles):
        for far in range(1, nh):
            tile_copy(i, far).wait_send()


def on_device(
    nh, nb,
    query_rows, key_rows, value_rows, residual, out_weight, attention_gate, norm_shift, norm_scale,
    expert_gate, expert_up, expert_down, routing, combine_weight,
):
    tok, width = query_rows.shape
    n = nh * nb
    cap = max(2, TOPK * tok // nb)
    sub = math.gcd(width // HD // nh, nb)
    gcols = width // (nh * sub)
    win = round_up(gcols, LANES)
    kvcols = round_up(2 * gcols, LANES)
    pieces = width // LANES
    block = cap * pieces
    ff = expert_up.shape[2]
    down_tile = math.gcd(width, 512)
    tiles = width // down_tile
    small = (
        query_rows, key_rows, value_rows, residual, attention_gate, norm_shift, norm_scale, expert_gate,
        routing.T, combine_weight.T,
    )
    vmem = pl.BlockSpec(memory_space=pltpu.VMEM)
    anywhere = pl.BlockSpec(memory_space=pl.ANY)
    return pl.pallas_call(
        functools.partial(kernel, (nh, nb, sub, cap)),
        out_shape=jax.ShapeDtypeStruct((tok, width), BF16),
        in_specs=[anywhere] * 13,
        out_specs=vmem,
        scratch_shapes=[
            *[pltpu.VMEM(array.shape, array.dtype) for array in small],
            pltpu.VMEM(out_weight.shape, BF16),
            pltpu.VMEM(expert_up.shape[1:], BF16),
            pltpu.VMEM(expert_down.shape[1:], BF16),
            pltpu.VMEM((nh * sub, tok, kvcols), BF16),
            pltpu.VMEM((2, n // 2, tok, kvcols), BF16),
            pltpu.VMEM((nh * sub, tok, win), BF16),
            pltpu.VMEM((nh * sub, tok, win), BF16),
            pltpu.VMEM((sub, nh * tok, win), BF16),
            pltpu.VMEM((sub, nh * tok, win), BF16),
            pltpu.VMEM((nh, tok, width), BF16),
            pltpu.VMEM((nh, tok, width), BF16),
            pltpu.VMEM((nb, block, LANES), BF16),
            pltpu.VMEM((n, block, LANES), BF16),
            pltpu.VMEM((tiles, nh, nb * cap, down_tile), BF16),
            pltpu.VMEM((tiles, nh - 1, nb * cap, down_tile), BF16),
            pltpu.VMEM((nb, block, LANES), BF16),
            pltpu.VMEM((nb, block, LANES), BF16),
            pltpu.VMEM((tok, width), F32),
            pltpu.VMEM((n * block, LANES), F32),
            pltpu.VMEM((nb * block, LANES), F32),
            pltpu.VMEM((n * cap, ff), BF16),
            pltpu.VMEM((n * cap, width), BF16),
            pltpu.SemaphoreType.DMA((len(small),)),
            pltpu.SemaphoreType.DMA((3,)),
            pltpu.SemaphoreType.DMA((7,)),
            pltpu.SemaphoreType.DMA((7,)),
            pltpu.SemaphoreType.DMA((tiles, nh - 1)),
            pltpu.SemaphoreType.DMA((tiles, nh - 1)),
        ],
        compiler_params=pltpu.CompilerParams(
            collective_id=0, has_side_effects=True, vmem_limit_bytes=60 * 1024 * 1024
        ),
        name="layer",
    )(*small, out_weight, expert_up, expert_down)


def solution(mesh):
    tokens = P(("head", "blk"), None)
    in_specs = (
        tokens, tokens, tokens, tokens,
        P("head", None), P(), P(), P(), P(),
        P("blk", None, "head"), P("blk", "head", None), tokens, tokens,
    )
    return jax.shard_map(
        functools.partial(on_device, mesh.shape["head"], mesh.shape["blk"]),
        mesh=mesh, in_specs=in_specs, out_specs=tokens, check_vma=False,
    )
```

```python
import functools
import math

import jax
import jax.numpy as jnp
from jax import lax
from jax.experimental import pallas as pl
from jax.experimental.pallas import tpu as pltpu
from jax.sharding import PartitionSpec as P

HD = 64
TOPK = 2
LANES = 128
MESH = pl.DeviceIdType.MESH
F32 = jnp.float32
BF16 = jnp.bfloat16


def round_up(value, step):
    return -(-value // step) * step


def dot(left, right):
    return lax.dot_general(left, right, (((1,), (0,)), ((), ())), preferred_element_type=F32)


def dot_nt(left, right):
    return lax.dot_general(left, right, (((1,), (1,)), ((), ())), preferred_element_type=F32)


def dot_tn(left, right):
    return lax.dot_general(left, right, (((0,), (0,)), ((), ())), preferred_element_type=F32)


def wrap(index, size):
    return jnp.where(index >= size, index - size, index)


def wait_bytes(ref, sem):
    pltpu.make_async_copy(ref, ref, sem).wait()


def kernel(
    dims,
    q_hbm, k_hbm, v_hbm, res_hbm, ag_hbm, shift_hbm, scale_hbm, eg_hbm, route_hbm, comb_hbm,
    ow_hbm, up_hbm, down_hbm,
    out_ref,
    q_ref, k_ref, v_ref, res_ref, ag_ref, shift_ref, scale_ref, eg_ref, route_ref, comb_ref,
    ow, up, down,
    kvs, kvr, qs, qr, ats, atr, ps, pr,
    mid, wide, thin, hidden, held,
    isem, wsem, ssem, rsem, csem,
    *chunked,
):
    sb, xr, eb, rr, flat = (chunked[i::5] for i in range(5))
    chunks = len(sb)
    nh, nb, sub, cap = dims
    n = nh * nb
    quarter = nb // sub
    tok, width = q_ref.shape
    gcols = width // (nh * sub)
    heads = gcols // HD
    win = qs.shape[2]
    kvcols = kvs.shape[2]
    klo = kvcols - win
    pieces = width // LANES
    h = lax.axis_index("head")
    b = lax.axis_index("blk")
    me = h * nb + b
    k_own = lax.div(b, quarter)
    m_own = b - k_own * quarter
    side = lax.rem(b, 2)
    half = n // 2
    half_me = h * (nb // 2) + lax.div(b, 2)

    inputs = [
        pltpu.make_async_copy(source, target, isem.at[i])
        for i, (source, target) in enumerate((
            (v_hbm, v_ref), (k_hbm, k_ref), (q_hbm, q_ref), (res_hbm, res_ref), (ag_hbm, ag_ref),
            (shift_hbm, shift_ref), (scale_hbm, scale_ref), (eg_hbm, eg_ref), (route_hbm, route_ref),
            (comb_hbm, comb_ref),
        ))
    ]
    for copy in inputs:
        copy.start()
    fetch = [
        pltpu.make_async_copy(ow_hbm, ow, wsem.at[0]),
        pltpu.make_async_copy(up_hbm.at[0], up, wsem.at[1]),
        pltpu.make_async_copy(down_hbm.at[0], down, wsem.at[2]),
    ]
    for copy in fetch:
        copy.start()

    barrier = pltpu.get_barrier_semaphore()

    def each_other(act):
        paired = nb & (nb - 1) == 0
        for far in reversed(range(nh)):
            to_h = wrap(h + far, nh)

            def step_to(step, carry, to_h=to_h):
                act(to_h, lax.bitwise_xor(b, nb - 1 - step) if paired else wrap(b + nb - 1 - step, nb))
                return carry

            lax.fori_loop(0, nb - 1 if far == 0 else nb, step_to, 0, unroll=nb <= 16)

    def greet(to_h, to_b):
        pl.semaphore_signal(barrier, inc=1, device_id=(to_h, to_b), device_id_type=MESH)

    each_other(greet)

    for copy in inputs:
        copy.wait()

    for g in range(nh * sub):
        cols = slice(g * gcols, (g + 1) * gcols)
        kvs[g, :, 0:gcols] = v_ref[:, cols]
        kvs[g, :, kvcols - gcols:kvcols] = k_ref[:, cols]
        if kvcols > 2 * gcols:
            kvs[g, :, gcols:kvcols - gcols] = jnp.zeros((tok, kvcols - 2 * gcols), BF16)
        if win > gcols:
            qs[g, :, 0:win - gcols] = jnp.zeros((tok, win - gcols), BF16)
        qs[g, :, win - gcols:win] = q_ref[:, cols]

    pl.semaphore_wait(barrier, n - 1)

    def remote(src, dst, phase, to_h, to_b, sends=ssem, receives=rsem):
        pltpu.make_async_remote_copy(
            src_ref=src, dst_ref=dst, send_sem=sends.at[phase], recv_sem=receives.at[phase],
            device_id=(to_h, to_b), device_id_type=MESH,
        ).start()

    def scatter(source_of, target, row):
        each_other(
            lambda to_h, to_b: remote(source_of(to_h, to_b), target.at[me], row, to_h, to_b, csem.at[0], csem.at[1])
        )
        pltpu.make_async_copy(source_of(h, b), target.at[me], csem.at[1, row]).start()

    def local(src, dst, phase):
        pltpu.make_async_copy(src, dst, rsem.at[phase]).start()

    for far in range(nh):
        to_h = wrap(h + far, nh)
        for step in range(sub):
            to_s = wrap(k_own + step, sub)
            source, target = qs.at[to_h * sub + to_s], qr.at[k_own * nh + h]
            if far == 0 and step == 0:
                local(source, target, 1)
            else:
                remote(source, target, 1, to_h, to_s * quarter + m_own)

    for far in range(nh):
        to_h = wrap(h + far, nh)

        def send_kv(step, carry, to_h=to_h):
            to_b = wrap(b + 2 * step, nb)
            source = kvs.at[to_h * sub + lax.div(to_b, quarter)]
            remote(source, kvr.at[side, half_me], 0, to_h, to_b)
            return carry

        lax.fori_loop(1 if far == 0 else 0, nb // 2, send_kv, 0, unroll=nb <= 16)
    local(kvs.at[h * sub + k_own], kvr.at[side, half_me], 0)

    slots = nb * cap
    row = lax.broadcasted_iota(jnp.int32, (slots, tok), 0)
    expert = row // cap
    place = (row - expert * cap).astype(F32)
    first = route_ref[0:1, :] == expert
    second = route_ref[1:2, :] == expert
    named = jnp.where(first | second, 1.0, 0.0)
    tri = jnp.where(
        lax.broadcasted_iota(jnp.int32, (tok, tok), 0) < lax.broadcasted_iota(jnp.int32, (tok, tok), 1),
        1.0, 0.0,
    )
    earlier = dot(named.astype(BF16), tri.astype(BF16))
    here = earlier == place
    pick = [jnp.where(choice & here, 1.0, 0.0) for choice in (first, second)]
    eye = lax.broadcasted_iota(jnp.int32, (tok, tok), 0) == lax.broadcasted_iota(jnp.int32, (tok, tok), 1)

    wait_bytes(kvr.at[side], rsem.at[0])
    pltpu.make_async_remote_copy(
        src_ref=kvr.at[side], dst_ref=kvr.at[side], send_sem=ssem.at[6], recv_sem=rsem.at[6],
        device_id=(h, b + 1 - 2 * side), device_id_type=MESH,
    ).start()
    wait_bytes(qr, rsem.at[1])

    rows = nh * sub * tok
    queries = qr[...].reshape(rows, win)
    lane = lax.broadcasted_iota(jnp.int32, (rows, win), 1)
    lows = [win - gcols + j * HD for j in range(heads)]
    split_q = jnp.concatenate(
        [jnp.where((lane >= lo) & (lane < lo + HD), queries, jnp.zeros_like(queries)) for lo in lows], axis=0
    )

    def score_half(which):
        keys = kvr[which, :, :, klo:kvcols].reshape(half * tok, win)
        return dot_nt(split_q, keys) * (1.0 / math.sqrt(HD))

    near_scores = score_half(side)
    near_peak = jnp.max(near_scores, axis=1, keepdims=True)
    near_values = kvr[side, :, :, 0:win].reshape(half * tok, win)
    wait_bytes(kvr.at[1 - side], rsem.at[6])
    far_scores = score_half(1 - side)
    far_values = kvr[1 - side, :, :, 0:win].reshape(half * tok, win)
    peak = jnp.maximum(near_peak, jnp.max(far_scores, axis=1, keepdims=True))
    near = jnp.exp(near_scores - peak)
    far = jnp.exp(far_scores - peak)
    total = jnp.sum(near, axis=1, keepdims=True) + jnp.sum(far, axis=1, keepdims=True)
    stacked = (dot(near.astype(BF16), near_values) + dot(far.astype(BF16), far_values)) / total
    attended = jnp.zeros((rows, win), F32)
    for j in range(heads):
        attended = jnp.where(
            (lane >= j * HD) & (lane < (j + 1) * HD), stacked[j * rows:(j + 1) * rows], attended
        )
    ats[...] = attended.astype(BF16).reshape(sub, nh * tok, win)

    for step in range(1, sub):
        to_k = wrap(k_own + step, sub)
        remote(ats.at[to_k], atr.at[k_own], 2, h, to_k * quarter + m_own)
    local(ats.at[k_own], atr.at[k_own], 2)
    fetch[0].wait()
    wait_bytes(atr, rsem.at[2])

    partial = jnp.zeros((nh * tok, width), F32)
    for s in range(sub):
        partial = partial + dot(atr[s, :, 0:gcols], ow[s * gcols:(s + 1) * gcols, :])
    ps[...] = partial.astype(BF16).reshape(nh, tok, width)

    for far in range(1, nh):
        to_h = wrap(h + far, nh)
        remote(ps.at[to_h], pr.at[h], 3, to_h, b)
    local(ps.at[h], pr.at[h], 3)
    wait_bytes(pr, rsem.at[3])

    projected = jnp.sum(pr[...].astype(F32), axis=0)
    middle = res_ref[...].astype(F32) + ag_ref[...] * projected
    average = jnp.mean(middle, axis=1, keepdims=True)
    centered = middle - average
    variance = jnp.mean(centered * centered, axis=1, keepdims=True)
    normed = (
        centered * lax.rsqrt(variance + 1e-06) * (1.0 + scale_ref[...]) + shift_ref[...]
    ).astype(BF16)
    mid[...] = middle

    spans = []
    for ref in sb:
        start = spans[-1][1] if spans else 0
        spans.append((start, start + ref.shape[1] // cap * LANES))
    buffer = dot((pick[0] + pick[1]).astype(BF16), normed)
    for i, (start, stop) in enumerate(spans):
        count = (stop - start) // LANES
        for c in range(count):
            thin[pl.ds(c, slots, count), :] = buffer[:, start + c * LANES:start + (c + 1) * LANES]
        sb[i][...] = thin[0:slots * count].reshape(sb[i].shape).astype(BF16)
        scatter(lambda to_h, to_b: sb[i].at[to_b], xr[i], i)

    ff = up.shape[1]
    up_tile = math.gcd(ff, 512)
    fetch[1].wait()
    for i, (start, stop) in enumerate(spans):
        count = (stop - start) // LANES
        wait_bytes(xr[i], csem.at[1, i])
        wide[0:n * cap * count] = xr[i][...].astype(F32).reshape(n * cap * count, LANES)
        for c in range(count):
            flat[i][:, c * LANES:(c + 1) * LANES] = wide[pl.ds(c, n * cap, count), :].astype(BF16)

        def up_step(t, carry, i=i, start=start, stop=stop):
            cols = pl.ds(pl.multiple_of(t * up_tile, up_tile), up_tile)
            u = dot(flat[i][...], up[start:stop, cols])
            if i > 0:
                u = held[:, cols] + u
            if i < chunks - 1:
                held[:, cols] = u
            else:
                inner = math.sqrt(2.0 / math.pi) * (u + 0.044715 * (u * u * u))
                hidden[:, cols] = (0.5 * u * (1.0 + jnp.tanh(inner))).astype(BF16)
            return carry

        lax.fori_loop(0, ff // up_tile, up_step, 0)

    fetch[2].wait()
    for i, (start, stop) in enumerate(spans):
        count = (stop - start) // LANES
        part = dot(hidden[...], down[:, start:stop])
        for c in range(count):
            wide[pl.ds(c, n * cap, count), :] = part[:, c * LANES:(c + 1) * LANES]
        eb[i][...] = wide[0:n * cap * count].reshape(eb[i].shape).astype(BF16)
        scatter(lambda to_h, to_b: eb[i].at[to_h * nb + to_b], rr[i], chunks + i)

    wait_bytes(kvr.at[0, pl.ds(0, half - 1)], ssem.at[0])
    wait_bytes(kvr.at[side], ssem.at[6])
    wait_bytes(qr.at[pl.ds(0, nh * sub - 1)], ssem.at[1])
    if sub > 1:
        wait_bytes(atr.at[pl.ds(0, sub - 1)], ssem.at[2])
    wait_bytes(pr.at[pl.ds(0, nh - 1)], ssem.at[3])
    weights = [
        jnp.sum(jnp.where(eye, comb_ref[i:i + 1, :], 0.0), axis=1, keepdims=True) for i in range(TOPK)
    ]
    for i, (start, stop) in enumerate(spans):
        count = (stop - start) // LANES
        wait_bytes(xr[i].at[pl.ds(0, n - 1)], csem.at[0, i])
        wait_bytes(rr[i], csem.at[1, chunks + i])
        summed = rr[i][0:nb].astype(F32)
        for other in range(1, nh):
            summed = summed + rr[i][other * nb:(other + 1) * nb].astype(F32)
        thin[0:slots * count] = summed.reshape(slots * count, LANES)
        back = jnp.concatenate(
            [thin[pl.ds(c, slots, count), :].astype(BF16) for c in range(count)], axis=1
        )
        mixture = weights[0] * dot_tn(pick[0].astype(BF16), back)
        mixture = mixture + weights[1] * dot_tn(pick[1].astype(BF16), back)
        out_ref[:, start:stop] = mid[:, start:stop] + eg_ref[start:stop] * mixture
    for i in range(chunks):
        wait_bytes(rr[i].at[pl.ds(0, n - 1)], csem.at[0, chunks + i])


def on_device(
    nh, nb,
    query_rows, key_rows, value_rows, residual, out_weight, attention_gate, norm_shift, norm_scale,
    expert_gate, expert_up, expert_down, routing, combine_weight,
):
    tok, width = query_rows.shape
    n = nh * nb
    cap = max(2, TOPK * tok // nb)
    sub = math.gcd(width // HD // nh, nb)
    gcols = width // (nh * sub)
    win = round_up(gcols, LANES)
    kvcols = round_up(2 * gcols, LANES)
    pieces = width // LANES
    last = max(1, pieces // 12) * 4 if pieces % 4 == 0 and pieces > 4 else 0
    counts = [count for count in (pieces - last, last) if count]
    most = max(counts) * cap
    ff = expert_up.shape[2]
    small = (
        query_rows, key_rows, value_rows, residual, attention_gate, norm_shift, norm_scale, expert_gate,
        routing.T, combine_weight.T,
    )
    vmem = pl.BlockSpec(memory_space=pltpu.VMEM)
    anywhere = pl.BlockSpec(memory_space=pl.ANY)
    return pl.pallas_call(
        functools.partial(kernel, (nh, nb, sub, cap)),
        out_shape=jax.ShapeDtypeStruct((tok, width), F32),
        in_specs=[anywhere] * 13,
        out_specs=vmem,
        scratch_shapes=[
            *[pltpu.VMEM(array.shape, array.dtype) for array in small],
            pltpu.VMEM(out_weight.shape, BF16),
            pltpu.VMEM(expert_up.shape[1:], BF16),
            pltpu.VMEM(expert_down.shape[1:], BF16),
            pltpu.VMEM((nh * sub, tok, kvcols), BF16),
            pltpu.VMEM((2, n // 2, tok, kvcols), BF16),
            pltpu.VMEM((nh * sub, tok, win), BF16),
            pltpu.VMEM((nh * sub, tok, win), BF16),
            pltpu.VMEM((sub, nh * tok, win), BF16),
            pltpu.VMEM((sub, nh * tok, win), BF16),
            pltpu.VMEM((nh, tok, width), BF16),
            pltpu.VMEM((nh, tok, width), BF16),
            pltpu.VMEM((tok, width), F32),
            pltpu.VMEM((n * most, LANES), F32),
            pltpu.VMEM((nb * most, LANES), F32),
            pltpu.VMEM((n * cap, ff), BF16),
            pltpu.VMEM((n * cap, ff), F32),
            pltpu.SemaphoreType.DMA((len(small),)),
            pltpu.SemaphoreType.DMA((3,)),
            pltpu.SemaphoreType.DMA((7,)),
            pltpu.SemaphoreType.DMA((7,)),
            pltpu.SemaphoreType.DMA((2, 2 * len(counts))),
            *[
                shape
                for count in counts
                for shape in (
                    pltpu.VMEM((nb, cap * count, LANES), BF16),
                    pltpu.VMEM((n, cap * count, LANES), BF16),
                    pltpu.VMEM((n, cap * count, LANES), BF16),
                    pltpu.VMEM((n, cap * count, LANES), BF16),
                    pltpu.VMEM((n * cap, count * LANES), BF16),
                )
            ],
        ],
        compiler_params=pltpu.CompilerParams(
            collective_id=0, has_side_effects=True, vmem_limit_bytes=60 * 1024 * 1024
        ),
        name="layer",
    )(*small, out_weight, expert_up, expert_down).astype(BF16)


def solution(mesh):
    tokens = P(("head", "blk"), None)
    in_specs = (
        tokens, tokens, tokens, tokens,
        P("head", None), P(), P(), P(), P(),
        P("blk", None, "head"), P("blk", "head", None), tokens, tokens,
    )
    return jax.shard_map(
        functools.partial(on_device, mesh.shape["head"], mesh.shape["blk"]),
        mesh=mesh, in_specs=in_specs, out_specs=tokens, check_vma=False,
    )
```

```python
import functools
import math

import jax
import jax.numpy as jnp
from jax import lax
from jax.experimental import pallas as pl
from jax.experimental.pallas import tpu as pltpu
from jax.sharding import PartitionSpec as P

HD = 64
TOPK = 2
LANES = 128
MESH = pl.DeviceIdType.MESH
F32 = jnp.float32
BF16 = jnp.bfloat16


def round_up(value, step):
    return -(-value // step) * step


def dot(left, right):
    return lax.dot_general(left, right, (((1,), (0,)), ((), ())), preferred_element_type=F32)


def dot_nt(left, right):
    return lax.dot_general(left, right, (((1,), (1,)), ((), ())), preferred_element_type=F32)


def dot_tn(left, right):
    return lax.dot_general(left, right, (((0,), (0,)), ((), ())), preferred_element_type=F32)


def wrap(index, size):
    return jnp.where(index >= size, index - size, index)


def wait_bytes(ref, sem):
    pltpu.make_async_copy(ref, ref, sem).wait()


def kernel(
    dims,
    q_hbm, k_hbm, v_hbm, res_hbm, ag_hbm, shift_hbm, scale_hbm, eg_hbm, route_hbm, comb_hbm,
    ow_hbm, up_hbm, down_hbm,
    out_ref,
    q_ref, k_ref, v_ref, res_ref, ag_ref, shift_ref, scale_ref, eg_ref, route_ref, comb_ref,
    ow, up, down,
    kvs, kvr, qs, qr, ats, atr, ps, pr,
    mid, wide, thin, hidden, held,
    isem, wsem, ssem, rsem, csem, psem,
    *chunked,
):
    sb, xr, eb, rr, flat = (chunked[i::5] for i in range(5))
    chunks = len(sb)
    nh, nb, sub, cap = dims
    n = nh * nb
    quarter = nb // sub
    tok, width = q_ref.shape
    gcols = width // (nh * sub)
    heads = gcols // HD
    win = qs.shape[2]
    kvcols = kvs.shape[2]
    klo = kvcols - win
    pieces = width // LANES
    h = lax.axis_index("head")
    b = lax.axis_index("blk")
    me = h * nb + b
    k_own = lax.div(b, quarter)
    m_own = b - k_own * quarter
    side = lax.rem(b, 2)
    half = n // 2
    half_me = h * (nb // 2) + lax.div(b, 2)

    barrier = pltpu.get_barrier_semaphore()

    def each_other(act):
        paired = nb & (nb - 1) == 0
        for far in reversed(range(nh)):
            to_h = wrap(h + far, nh)

            def step_to(step, carry, to_h=to_h):
                act(to_h, lax.bitwise_xor(b, nb - 1 - step) if paired else wrap(b + nb - 1 - step, nb))
                return carry

            lax.fori_loop(0, nb - 1 if far == 0 else nb, step_to, 0, unroll=nb <= 16)

    def greet(to_h, to_b):
        pl.semaphore_signal(barrier, inc=1, device_id=(to_h, to_b), device_id_type=MESH)

    each_other(greet)

    inputs = [
        pltpu.make_async_copy(source, target, isem.at[i])
        for i, (source, target) in enumerate((
            (v_hbm, v_ref), (k_hbm, k_ref), (q_hbm, q_ref), (res_hbm, res_ref), (ag_hbm, ag_ref),
            (shift_hbm, shift_ref), (scale_hbm, scale_ref), (eg_hbm, eg_ref), (route_hbm, route_ref),
            (comb_hbm, comb_ref),
        ))
    ]
    for copy in inputs:
        copy.start()
    fetch = [
        pltpu.make_async_copy(ow_hbm, ow, wsem.at[0]),
        pltpu.make_async_copy(up_hbm.at[0], up, wsem.at[1]),
        pltpu.make_async_copy(down_hbm.at[0], down, wsem.at[2]),
    ]
    for copy in fetch:
        copy.start()

    for copy in inputs[:2]:
        copy.wait()
    for g in range(nh * sub):
        cols = slice(g * gcols, (g + 1) * gcols)
        kvs[g, :, 0:gcols] = v_ref[:, cols]
        kvs[g, :, kvcols - gcols:kvcols] = k_ref[:, cols]
        if kvcols > 2 * gcols:
            kvs[g, :, gcols:kvcols - gcols] = jnp.zeros((tok, kvcols - 2 * gcols), BF16)

    pl.semaphore_wait(barrier, n - 1)

    def remote(src, dst, phase, to_h, to_b, sends=ssem, receives=rsem):
        pltpu.make_async_remote_copy(
            src_ref=src, dst_ref=dst, send_sem=sends.at[phase], recv_sem=receives.at[phase],
            device_id=(to_h, to_b), device_id_type=MESH,
        ).start()

    def scatter(source_of, target, row):
        each_other(
            lambda to_h, to_b: remote(source_of(to_h, to_b), target.at[me], row, to_h, to_b, csem.at[0], csem.at[1])
        )
        pltpu.make_async_copy(source_of(h, b), target.at[me], csem.at[1, row]).start()

    def local(src, dst, phase):
        pltpu.make_async_copy(src, dst, rsem.at[phase]).start()

    for far in range(nh):
        to_h = wrap(h + far, nh)

        def send_kv(step, carry, to_h=to_h):
            to_b = wrap(b + 2 * step, nb)
            source = kvs.at[to_h * sub + lax.div(to_b, quarter)]
            remote(source, kvr.at[side, half_me], 0, to_h, to_b)
            return carry

        lax.fori_loop(1 if far == 0 else 0, nb // 2, send_kv, 0, unroll=nb <= 16)
    local(kvs.at[h * sub + k_own], kvr.at[side, half_me], 0)

    inputs[2].wait()
    for g in range(nh * sub):
        cols = slice(g * gcols, (g + 1) * gcols)
        if win > gcols:
            qs[g, :, 0:win - gcols] = jnp.zeros((tok, win - gcols), BF16)
        qs[g, :, win - gcols:win] = q_ref[:, cols]
    for far in range(nh):
        to_h = wrap(h + far, nh)
        for step in range(sub):
            to_s = wrap(k_own + step, sub)
            source, target = qs.at[to_h * sub + to_s], qr.at[k_own * nh + h]
            if far == 0 and step == 0:
                local(source, target, 1)
            else:
                remote(source, target, 1, to_h, to_s * quarter + m_own)

    for copy in inputs[3:]:
        copy.wait()

    slots = nb * cap
    row = lax.broadcasted_iota(jnp.int32, (slots, tok), 0)
    expert = row // cap
    place = (row - expert * cap).astype(F32)
    first = route_ref[0:1, :] == expert
    second = route_ref[1:2, :] == expert
    named = jnp.where(first | second, 1.0, 0.0)
    tri = jnp.where(
        lax.broadcasted_iota(jnp.int32, (tok, tok), 0) < lax.broadcasted_iota(jnp.int32, (tok, tok), 1),
        1.0, 0.0,
    )
    earlier = dot(named.astype(BF16), tri.astype(BF16))
    here = earlier == place
    pick = [jnp.where(choice & here, 1.0, 0.0) for choice in (first, second)]
    eye = lax.broadcasted_iota(jnp.int32, (tok, tok), 0) == lax.broadcasted_iota(jnp.int32, (tok, tok), 1)

    wait_bytes(kvr.at[side], rsem.at[0])
    pltpu.make_async_remote_copy(
        src_ref=kvr.at[side], dst_ref=kvr.at[side], send_sem=ssem.at[6], recv_sem=rsem.at[6],
        device_id=(h, b + 1 - 2 * side), device_id_type=MESH,
    ).start()
    wait_bytes(qr, rsem.at[1])

    rows = nh * sub * tok
    queries = qr[...].reshape(rows, win)
    lane = lax.broadcasted_iota(jnp.int32, (rows, win), 1)
    lows = [win - gcols + j * HD for j in range(heads)]
    split_q = jnp.concatenate(
        [jnp.where((lane >= lo) & (lane < lo + HD), queries, jnp.zeros_like(queries)) for lo in lows], axis=0
    )

    def score_half(which):
        keys = kvr[which, :, :, klo:kvcols].reshape(half * tok, win)
        return dot_nt(split_q, keys) * (1.0 / math.sqrt(HD))

    near_scores = score_half(side)
    near_peak = jnp.max(near_scores, axis=1, keepdims=True)
    near_values = kvr[side, :, :, 0:win].reshape(half * tok, win)
    wait_bytes(kvr.at[1 - side], rsem.at[6])
    far_scores = score_half(1 - side)
    far_values = kvr[1 - side, :, :, 0:win].reshape(half * tok, win)
    peak = jnp.maximum(near_peak, jnp.max(far_scores, axis=1, keepdims=True))
    near = jnp.exp(near_scores - peak)
    far = jnp.exp(far_scores - peak)
    total = jnp.sum(near, axis=1, keepdims=True) + jnp.sum(far, axis=1, keepdims=True)
    stacked = (dot(near.astype(BF16), near_values) + dot(far.astype(BF16), far_values)) / total
    attended = jnp.zeros((rows, win), F32)
    for j in range(heads):
        attended = jnp.where(
            (lane >= j * HD) & (lane < (j + 1) * HD), stacked[j * rows:(j + 1) * rows], attended
        )
    ats[...] = attended.astype(BF16).reshape(sub, nh * tok, win)

    for step in range(1, sub):
        to_k = wrap(k_own + step, sub)
        remote(ats.at[to_k], atr.at[k_own], 2, h, to_k * quarter + m_own)
    local(ats.at[k_own], atr.at[k_own], 2)
    fetch[0].wait()
    wait_bytes(atr, rsem.at[2])

    splits, _, _, part_tile = ps.shape

    def part_copy(i, far):
        to_h = wrap(h + far, nh)
        return pltpu.make_async_remote_copy(
            src_ref=ps.at[i, to_h], dst_ref=pr.at[i, far - 1], send_sem=psem.at[0, i, far - 1],
            recv_sem=psem.at[1, i, far - 1], device_id=(to_h, b), device_id_type=MESH,
        )

    for i in range(splits):
        partial = jnp.zeros((nh * tok, part_tile), F32)
        for s in range(sub):
            partial = partial + dot(
                atr[s, :, 0:gcols], ow[s * gcols:(s + 1) * gcols, i * part_tile:(i + 1) * part_tile]
            )
        ps[i] = partial.astype(BF16).reshape(nh, tok, part_tile)
        for far in range(1, nh):
            part_copy(i, far).start()
    sums = []
    for i in range(splits):
        both = ps[i, h].astype(F32)
        for far in range(1, nh):
            part_copy(i, far).wait_recv()
            both = both + pr[i, far - 1].astype(F32)
        sums.append(both)
    projected = jnp.concatenate(sums, axis=1)
    middle = res_ref[...].astype(F32) + ag_ref[...] * projected
    average = jnp.mean(middle, axis=1, keepdims=True)
    centered = middle - average
    variance = jnp.mean(centered * centered, axis=1, keepdims=True)
    normed = (
        centered * lax.rsqrt(variance + 1e-06) * (1.0 + scale_ref[...]) + shift_ref[...]
    ).astype(BF16)
    mid[...] = middle

    spans = []
    for ref in sb:
        start = spans[-1][1] if spans else 0
        spans.append((start, start + ref.shape[1] // cap * LANES))
    buffer = dot((pick[0] + pick[1]).astype(BF16), normed)
    for i, (start, stop) in enumerate(spans):
        count = (stop - start) // LANES
        for c in range(count):
            thin[pl.ds(c, slots, count), :] = buffer[:, start + c * LANES:start + (c + 1) * LANES]
        sb[i][...] = thin[0:slots * count].reshape(sb[i].shape).astype(BF16)
        scatter(lambda to_h, to_b: sb[i].at[to_b], xr[i], i)

    ff = up.shape[1]
    up_tile = math.gcd(ff, 512)
    fetch[1].wait()
    for i, (start, stop) in enumerate(spans):
        count = (stop - start) // LANES
        wait_bytes(xr[i], csem.at[1, i])
        wide[0:n * cap * count] = xr[i][...].astype(F32).reshape(n * cap * count, LANES)
        for c in range(count):
            flat[i][:, c * LANES:(c + 1) * LANES] = wide[pl.ds(c, n * cap, count), :].astype(BF16)

        def up_step(t, carry, i=i, start=start, stop=stop):
            cols = pl.ds(pl.multiple_of(t * up_tile, up_tile), up_tile)
            u = dot(flat[i][...], up[start:stop, cols])
            if i > 0:
                u = held[:, cols] + u
            if i < chunks - 1:
                held[:, cols] = u
            else:
                inner = math.sqrt(2.0 / math.pi) * (u + 0.044715 * (u * u * u))
                hidden[:, cols] = (0.5 * u * (1.0 + jnp.tanh(inner))).astype(BF16)
            return carry

        lax.fori_loop(0, ff // up_tile, up_step, 0)

    fetch[2].wait()
    for i, (start, stop) in enumerate(spans):
        count = (stop - start) // LANES
        part = dot(hidden[...], down[:, start:stop])
        for c in range(count):
            wide[pl.ds(c, n * cap, count), :] = part[:, c * LANES:(c + 1) * LANES]
        eb[i][...] = wide[0:n * cap * count].reshape(eb[i].shape).astype(BF16)
        scatter(lambda to_h, to_b: eb[i].at[to_h * nb + to_b], rr[i], chunks + i)

    wait_bytes(kvr.at[0, pl.ds(0, half - 1)], ssem.at[0])
    wait_bytes(kvr.at[side], ssem.at[6])
    wait_bytes(qr.at[pl.ds(0, nh * sub - 1)], ssem.at[1])
    if sub > 1:
        wait_bytes(atr.at[pl.ds(0, sub - 1)], ssem.at[2])
    for i in range(splits):
        for far in range(1, nh):
            part_copy(i, far).wait_send()
    weights = [
        jnp.sum(jnp.where(eye, comb_ref[i:i + 1, :], 0.0), axis=1, keepdims=True) for i in range(TOPK)
    ]
    for i, (start, stop) in enumerate(spans):
        count = (stop - start) // LANES
        wait_bytes(xr[i].at[pl.ds(0, n - 1)], csem.at[0, i])
        wait_bytes(rr[i], csem.at[1, chunks + i])
        summed = rr[i][0:nb].astype(F32)
        for other in range(1, nh):
            summed = summed + rr[i][other * nb:(other + 1) * nb].astype(F32)
        thin[0:slots * count] = summed.reshape(slots * count, LANES)
        back = jnp.concatenate(
            [thin[pl.ds(c, slots, count), :].astype(BF16) for c in range(count)], axis=1
        )
        mixture = weights[0] * dot_tn(pick[0].astype(BF16), back)
        mixture = mixture + weights[1] * dot_tn(pick[1].astype(BF16), back)
        out_ref[:, start:stop] = mid[:, start:stop] + eg_ref[start:stop] * mixture
    for i in range(chunks):
        wait_bytes(rr[i].at[pl.ds(0, n - 1)], csem.at[0, chunks + i])


def on_device(
    nh, nb,
    query_rows, key_rows, value_rows, residual, out_weight, attention_gate, norm_shift, norm_scale,
    expert_gate, expert_up, expert_down, routing, combine_weight,
):
    tok, width = query_rows.shape
    n = nh * nb
    cap = max(2, TOPK * tok // nb)
    sub = math.gcd(width // HD // nh, nb)
    gcols = width // (nh * sub)
    win = round_up(gcols, LANES)
    kvcols = round_up(2 * gcols, LANES)
    pieces = width // LANES
    part_tile = math.gcd(width, 768)
    splits = width // part_tile
    last = max(1, pieces // 12) * 4 if pieces % 4 == 0 and pieces > 4 else 0
    counts = [count for count in (pieces - last, last) if count]
    most = max(counts) * cap
    ff = expert_up.shape[2]
    small = (
        query_rows, key_rows, value_rows, residual, attention_gate, norm_shift, norm_scale, expert_gate,
        routing.T, combine_weight.T,
    )
    vmem = pl.BlockSpec(memory_space=pltpu.VMEM)
    anywhere = pl.BlockSpec(memory_space=pl.ANY)
    return pl.pallas_call(
        functools.partial(kernel, (nh, nb, sub, cap)),
        out_shape=pltpu.VMEM((tok, width), F32),
        in_specs=[anywhere] * 13,
        out_specs=vmem,
        scratch_shapes=[
            *[pltpu.VMEM(array.shape, array.dtype) for array in small],
            pltpu.VMEM(out_weight.shape, BF16),
            pltpu.VMEM(expert_up.shape[1:], BF16),
            pltpu.VMEM(expert_down.shape[1:], BF16),
            pltpu.VMEM((nh * sub, tok, kvcols), BF16),
            pltpu.VMEM((2, n // 2, tok, kvcols), BF16),
            pltpu.VMEM((nh * sub, tok, win), BF16),
            pltpu.VMEM((nh * sub, tok, win), BF16),
            pltpu.VMEM((sub, nh * tok, win), BF16),
            pltpu.VMEM((sub, nh * tok, win), BF16),
            pltpu.VMEM((splits, nh, tok, part_tile), BF16),
            pltpu.VMEM((splits, nh - 1, tok, part_tile), BF16),
            pltpu.VMEM((tok, width), F32),
            pltpu.VMEM((n * most, LANES), F32),
            pltpu.VMEM((nb * most, LANES), F32),
            pltpu.VMEM((n * cap, ff), BF16),
            pltpu.VMEM((n * cap, ff), F32),
            pltpu.SemaphoreType.DMA((len(small),)),
            pltpu.SemaphoreType.DMA((3,)),
            pltpu.SemaphoreType.DMA((7,)),
            pltpu.SemaphoreType.DMA((7,)),
            pltpu.SemaphoreType.DMA((2, 2 * len(counts))),
            pltpu.SemaphoreType.DMA((2, splits, nh - 1)),
            *[
                shape
                for count in counts
                for shape in (
                    pltpu.VMEM((nb, cap * count, LANES), BF16),
                    pltpu.VMEM((n, cap * count, LANES), BF16),
                    pltpu.VMEM((n, cap * count, LANES), BF16),
                    pltpu.VMEM((n, cap * count, LANES), BF16),
                    pltpu.VMEM((n * cap, count * LANES), BF16),
                )
            ],
        ],
        compiler_params=pltpu.CompilerParams(
            collective_id=0, has_side_effects=True, vmem_limit_bytes=60 * 1024 * 1024
        ),
        name="layer",
    )(*small, out_weight, expert_up, expert_down).astype(BF16)


def solution(mesh):
    tokens = P(("head", "blk"), None)
    in_specs = (
        tokens, tokens, tokens, tokens,
        P("head", None), P(), P(), P(), P(),
        P("blk", None, "head"), P("blk", "head", None), tokens, tokens,
    )
    return jax.shard_map(
        functools.partial(on_device, mesh.shape["head"], mesh.shape["blk"]),
        mesh=mesh, in_specs=in_specs, out_specs=tokens, check_vma=False,
    )
```

```python
import functools
import math

import jax
import jax.numpy as jnp
from jax import lax
from jax.experimental import pallas as pl
from jax.experimental.pallas import tpu as pltpu
from jax.sharding import PartitionSpec as P

HD = 64
TOPK = 2
LANES = 128
MESH = pl.DeviceIdType.MESH
F32 = jnp.float32
BF16 = jnp.bfloat16


def round_up(value, step):
    return -(-value // step) * step


def dot(left, right):
    return lax.dot_general(left, right, (((1,), (0,)), ((), ())), preferred_element_type=F32)


def dot_nt(left, right):
    return lax.dot_general(left, right, (((1,), (1,)), ((), ())), preferred_element_type=F32)


def dot_tn(left, right):
    return lax.dot_general(left, right, (((0,), (0,)), ((), ())), preferred_element_type=F32)


def wrap(index, size):
    return jnp.where(index >= size, index - size, index)


def wait_bytes(ref, sem):
    pltpu.make_async_copy(ref, ref, sem).wait()


def kernel(
    dims,
    q_hbm, k_hbm, v_hbm, res_hbm, ag_hbm, shift_hbm, scale_hbm, eg_hbm, route_hbm, comb_hbm,
    ow_hbm, up_hbm, down_hbm,
    out_ref,
    q_ref, k_ref, v_ref, res_ref, ag_ref, shift_ref, scale_ref, eg_ref, route_ref, comb_ref,
    ow, up, down,
    kvs, kvr, qs, qr, ats, atr, ps, pr,
    mid, wide, thin, hidden, held,
    isem, wsem, ssem, rsem, csem, psem,
    *chunked,
):
    sb, xr, eb, rr, flat = (chunked[i::5] for i in range(5))
    chunks = len(sb)
    nh, nb, sub, cap = dims
    n = nh * nb
    quarter = nb // sub
    tok, width = q_ref.shape
    gcols = width // (nh * sub)
    heads = gcols // HD
    win = qs.shape[2]
    kvcols = kvs.shape[2]
    klo = kvcols - win
    pieces = width // LANES
    h = lax.axis_index("head")
    b = lax.axis_index("blk")
    me = h * nb + b
    k_own = lax.div(b, quarter)
    m_own = b - k_own * quarter
    side = lax.rem(b, 2)
    half = n // 2
    half_me = h * (nb // 2) + lax.div(b, 2)

    barrier = pltpu.get_barrier_semaphore()

    def each_other(act):
        paired = nb & (nb - 1) == 0
        for far in reversed(range(nh)):
            to_h = wrap(h + far, nh)

            def step_to(step, carry, to_h=to_h):
                act(to_h, lax.bitwise_xor(b, nb - 1 - step) if paired else wrap(b + nb - 1 - step, nb))
                return carry

            lax.fori_loop(0, nb - 1 if far == 0 else nb, step_to, 0, unroll=nb <= 16)

    def greet(to_h, to_b):
        pl.semaphore_signal(barrier, inc=1, device_id=(to_h, to_b), device_id_type=MESH)

    each_other(greet)

    inputs = [
        pltpu.make_async_copy(source, target, isem.at[i])
        for i, (source, target) in enumerate((
            (v_hbm, v_ref), (k_hbm, k_ref), (q_hbm, q_ref), (res_hbm, res_ref), (ag_hbm, ag_ref),
            (shift_hbm, shift_ref), (scale_hbm, scale_ref), (eg_hbm, eg_ref), (route_hbm, route_ref),
            (comb_hbm, comb_ref),
        ))
    ]
    for copy in inputs:
        copy.start()
    fetch = [
        pltpu.make_async_copy(ow_hbm, ow, wsem.at[0]),
        pltpu.make_async_copy(up_hbm.at[0], up, wsem.at[1]),
        pltpu.make_async_copy(down_hbm.at[0], down, wsem.at[2]),
    ]
    for copy in fetch:
        copy.start()

    for copy in inputs[:2]:
        copy.wait()
    for g in range(nh * sub):
        cols = slice(g * gcols, (g + 1) * gcols)
        kvs[g, :, 0:gcols] = v_ref[:, cols]
        kvs[g, :, kvcols - gcols:kvcols] = k_ref[:, cols]
        if kvcols > 2 * gcols:
            kvs[g, :, gcols:kvcols - gcols] = jnp.zeros((tok, kvcols - 2 * gcols), BF16)

    pl.semaphore_wait(barrier, n - 1)

    def remote(src, dst, phase, to_h, to_b, sends=ssem, receives=rsem):
        pltpu.make_async_remote_copy(
            src_ref=src, dst_ref=dst, send_sem=sends.at[phase], recv_sem=receives.at[phase],
            device_id=(to_h, to_b), device_id_type=MESH,
        ).start()

    def scatter(source_of, target, row):
        each_other(
            lambda to_h, to_b: remote(source_of(to_h, to_b), target.at[me], row, to_h, to_b, csem.at[0], csem.at[1])
        )
        pltpu.make_async_copy(source_of(h, b), target.at[me], csem.at[1, row]).start()

    def local(src, dst, phase):
        pltpu.make_async_copy(src, dst, rsem.at[phase]).start()

    for far in range(nh):
        to_h = wrap(h + far, nh)

        def send_kv(step, carry, to_h=to_h):
            to_b = wrap(b + 2 * step, nb)
            source = kvs.at[to_h * sub + lax.div(to_b, quarter)]
            remote(source, kvr.at[side, half_me], 0, to_h, to_b)
            return carry

        lax.fori_loop(1 if far == 0 else 0, nb // 2, send_kv, 0, unroll=nb <= 16)
    local(kvs.at[h * sub + k_own], kvr.at[side, half_me], 0)

    inputs[2].wait()
    for g in range(nh * sub):
        cols = slice(g * gcols, (g + 1) * gcols)
        if win > gcols:
            qs[g, :, 0:win - gcols] = jnp.zeros((tok, win - gcols), BF16)
        qs[g, :, win - gcols:win] = q_ref[:, cols]
    for far in range(nh):
        to_h = wrap(h + far, nh)
        for step in range(sub):
            to_s = wrap(k_own + step, sub)
            source, target = qs.at[to_h * sub + to_s], qr.at[k_own * nh + h]
            if far == 0 and step == 0:
                local(source, target, 1)
            else:
                remote(source, target, 1, to_h, to_s * quarter + m_own)

    for copy in inputs[3:]:
        copy.wait()

    slots = nb * cap
    row = lax.broadcasted_iota(jnp.int32, (slots, tok), 0)
    expert = row // cap
    place = (row - expert * cap).astype(F32)
    first = route_ref[0:1, :] == expert
    second = route_ref[1:2, :] == expert
    named = jnp.where(first | second, 1.0, 0.0)
    tri = jnp.where(
        lax.broadcasted_iota(jnp.int32, (tok, tok), 0) < lax.broadcasted_iota(jnp.int32, (tok, tok), 1),
        1.0, 0.0,
    )
    earlier = dot(named.astype(BF16), tri.astype(BF16))
    here = earlier == place
    pick = [jnp.where(choice & here, 1.0, 0.0) for choice in (first, second)]
    eye = lax.broadcasted_iota(jnp.int32, (tok, tok), 0) == lax.broadcasted_iota(jnp.int32, (tok, tok), 1)

    wait_bytes(kvr.at[side], rsem.at[0])
    pltpu.make_async_remote_copy(
        src_ref=kvr.at[side], dst_ref=kvr.at[side], send_sem=ssem.at[6], recv_sem=rsem.at[6],
        device_id=(h, b + 1 - 2 * side), device_id_type=MESH,
    ).start()
    wait_bytes(qr, rsem.at[1])

    rows = nh * sub * tok
    queries = qr[...].reshape(rows, win)
    lane = lax.broadcasted_iota(jnp.int32, (rows, win), 1)
    lows = [win - gcols + j * HD for j in range(heads)]
    split_q = jnp.concatenate(
        [jnp.where((lane >= lo) & (lane < lo + HD), queries, jnp.zeros_like(queries)) for lo in lows], axis=0
    )

    def score_half(which):
        keys = kvr[which, :, :, klo:kvcols].reshape(half * tok, win)
        return dot_nt(split_q, keys) * (1.0 / math.sqrt(HD))

    near_scores = score_half(side)
    near_peak = jnp.max(near_scores, axis=1, keepdims=True)
    near_values = kvr[side, :, :, 0:win].reshape(half * tok, win)
    wait_bytes(kvr.at[1 - side], rsem.at[6])
    far_scores = score_half(1 - side)
    far_values = kvr[1 - side, :, :, 0:win].reshape(half * tok, win)
    peak = jnp.maximum(near_peak, jnp.max(far_scores, axis=1, keepdims=True))
    near = jnp.exp(near_scores - peak)
    far = jnp.exp(far_scores - peak)
    total = jnp.sum(near, axis=1, keepdims=True) + jnp.sum(far, axis=1, keepdims=True)
    stacked = (dot(near.astype(BF16), near_values) + dot(far.astype(BF16), far_values)) / total
    attended = jnp.zeros((rows, win), F32)
    for j in range(heads):
        attended = jnp.where(
            (lane >= j * HD) & (lane < (j + 1) * HD), stacked[j * rows:(j + 1) * rows], attended
        )
    ats[...] = attended.astype(BF16).reshape(sub, nh * tok, win)

    for step in range(1, sub):
        to_k = wrap(k_own + step, sub)
        remote(ats.at[to_k], atr.at[k_own], 2, h, to_k * quarter + m_own)
    local(ats.at[k_own], atr.at[k_own], 2)
    fetch[0].wait()
    wait_bytes(atr, rsem.at[2])

    splits, _, _, part_tile = ps.shape

    def part_copy(i, far):
        to_h = wrap(h + far, nh)
        return pltpu.make_async_remote_copy(
            src_ref=ps.at[i, to_h], dst_ref=pr.at[i, far - 1], send_sem=psem.at[0, i, far - 1],
            recv_sem=psem.at[1, i, far - 1], device_id=(to_h, b), device_id_type=MESH,
        )

    for i in range(splits):
        partial = jnp.zeros((nh * tok, part_tile), F32)
        for s in range(sub):
            partial = partial + dot(
                atr[s, :, 0:gcols], ow[s * gcols:(s + 1) * gcols, i * part_tile:(i + 1) * part_tile]
            )
        ps[i] = partial.astype(BF16).reshape(nh, tok, part_tile)
        for far in range(1, nh):
            part_copy(i, far).start()
    sums = []
    for i in range(splits):
        both = ps[i, h].astype(F32)
        for far in range(1, nh):
            part_copy(i, far).wait_recv()
            both = both + pr[i, far - 1].astype(F32)
        sums.append(both)
    projected = jnp.concatenate(sums, axis=1)
    middle = res_ref[...].astype(F32) + ag_ref[...] * projected
    average = jnp.mean(middle, axis=1, keepdims=True)
    centered = middle - average
    variance = jnp.mean(centered * centered, axis=1, keepdims=True)
    normed = (
        centered * lax.rsqrt(variance + 1e-06) * (1.0 + scale_ref[...]) + shift_ref[...]
    ).astype(BF16)
    mid[...] = middle

    spans = []
    for ref in sb:
        start = spans[-1][1] if spans else 0
        spans.append((start, start + ref.shape[1] // cap * LANES))
    buffer = dot((pick[0] + pick[1]).astype(BF16), normed)
    for i, (start, stop) in enumerate(spans):
        count = (stop - start) // LANES
        for c in range(count):
            thin[pl.ds(c, slots, count), :] = buffer[:, start + c * LANES:start + (c + 1) * LANES]
        sb[i][...] = thin[0:slots * count].reshape(sb[i].shape).astype(BF16)
        scatter(lambda to_h, to_b: sb[i].at[to_b], xr[i], i)

    ff = up.shape[1]
    up_tile = math.gcd(ff, 512)
    fetch[1].wait()
    for i, (start, stop) in enumerate(spans):
        count = (stop - start) // LANES
        wait_bytes(xr[i], csem.at[1, i])
        wide[0:n * cap * count] = xr[i][...].astype(F32).reshape(n * cap * count, LANES)
        for c in range(count):
            flat[i][:, c * LANES:(c + 1) * LANES] = wide[pl.ds(c, n * cap, count), :].astype(BF16)

        def up_step(t, carry, i=i, start=start, stop=stop):
            cols = pl.ds(pl.multiple_of(t * up_tile, up_tile), up_tile)
            u = dot(flat[i][...], up[start:stop, cols])
            if i > 0:
                u = held[:, cols] + u
            if i < chunks - 1:
                held[:, cols] = u
            else:
                inner = math.sqrt(2.0 / math.pi) * (u + 0.044715 * (u * u * u))
                hidden[:, cols] = (0.5 * u * (1.0 + jnp.tanh(inner))).astype(BF16)
            return carry

        lax.fori_loop(0, ff // up_tile, up_step, 0, unroll=True)

    fetch[2].wait()
    for i, (start, stop) in enumerate(spans):
        count = (stop - start) // LANES
        part = dot(hidden[...], down[:, start:stop])
        for c in range(count):
            wide[pl.ds(c, n * cap, count), :] = part[:, c * LANES:(c + 1) * LANES]
        eb[i][...] = wide[0:n * cap * count].reshape(eb[i].shape).astype(BF16)
        scatter(lambda to_h, to_b: eb[i].at[to_h * nb + to_b], rr[i], chunks + i)

    wait_bytes(kvr.at[0, pl.ds(0, half - 1)], ssem.at[0])
    wait_bytes(kvr.at[side], ssem.at[6])
    wait_bytes(qr.at[pl.ds(0, nh * sub - 1)], ssem.at[1])
    if sub > 1:
        wait_bytes(atr.at[pl.ds(0, sub - 1)], ssem.at[2])
    for i in range(splits):
        for far in range(1, nh):
            part_copy(i, far).wait_send()
    weights = [
        jnp.sum(jnp.where(eye, comb_ref[i:i + 1, :], 0.0), axis=1, keepdims=True) for i in range(TOPK)
    ]
    for i, (start, stop) in enumerate(spans):
        count = (stop - start) // LANES
        wait_bytes(xr[i].at[pl.ds(0, n - 1)], csem.at[0, i])
        wait_bytes(rr[i], csem.at[1, chunks + i])
        summed = rr[i][0:nb].astype(F32)
        for other in range(1, nh):
            summed = summed + rr[i][other * nb:(other + 1) * nb].astype(F32)
        thin[0:slots * count] = summed.reshape(slots * count, LANES)
        back = jnp.concatenate(
            [thin[pl.ds(c, slots, count), :].astype(BF16) for c in range(count)], axis=1
        )
        mixture = weights[0] * dot_tn(pick[0].astype(BF16), back)
        mixture = mixture + weights[1] * dot_tn(pick[1].astype(BF16), back)
        out_ref[:, start:stop] = mid[:, start:stop] + eg_ref[start:stop] * mixture
    for i in range(chunks):
        wait_bytes(rr[i].at[pl.ds(0, n - 1)], csem.at[0, chunks + i])


def on_device(
    nh, nb,
    query_rows, key_rows, value_rows, residual, out_weight, attention_gate, norm_shift, norm_scale,
    expert_gate, expert_up, expert_down, routing, combine_weight,
):
    tok, width = query_rows.shape
    n = nh * nb
    cap = max(2, TOPK * tok // nb)
    sub = math.gcd(width // HD // nh, nb)
    gcols = width // (nh * sub)
    win = round_up(gcols, LANES)
    kvcols = round_up(2 * gcols, LANES)
    pieces = width // LANES
    part_tile = math.gcd(width, 768)
    splits = width // part_tile
    last = max(1, pieces // 12) * 4 if pieces % 4 == 0 and pieces > 4 else 0
    counts = [count for count in (pieces - last, last) if count]
    most = max(counts) * cap
    ff = expert_up.shape[2]
    small = (
        query_rows, key_rows, value_rows, residual, attention_gate, norm_shift, norm_scale, expert_gate,
        routing.T, combine_weight.T,
    )
    vmem = pl.BlockSpec(memory_space=pltpu.VMEM)
    anywhere = pl.BlockSpec(memory_space=pl.ANY)
    return pl.pallas_call(
        functools.partial(kernel, (nh, nb, sub, cap)),
        out_shape=pltpu.VMEM((tok, width), F32),
        in_specs=[anywhere] * 13,
        out_specs=vmem,
        scratch_shapes=[
            *[pltpu.VMEM(array.shape, array.dtype) for array in small],
            pltpu.VMEM(out_weight.shape, BF16),
            pltpu.VMEM(expert_up.shape[1:], BF16),
            pltpu.VMEM(expert_down.shape[1:], BF16),
            pltpu.VMEM((nh * sub, tok, kvcols), BF16),
            pltpu.VMEM((2, n // 2, tok, kvcols), BF16),
            pltpu.VMEM((nh * sub, tok, win), BF16),
            pltpu.VMEM((nh * sub, tok, win), BF16),
            pltpu.VMEM((sub, nh * tok, win), BF16),
            pltpu.VMEM((sub, nh * tok, win), BF16),
            pltpu.VMEM((splits, nh, tok, part_tile), BF16),
            pltpu.VMEM((splits, nh - 1, tok, part_tile), BF16),
            pltpu.VMEM((tok, width), F32),
            pltpu.VMEM((n * most, LANES), F32),
            pltpu.VMEM((nb * most, LANES), F32),
            pltpu.VMEM((n * cap, ff), BF16),
            pltpu.VMEM((n * cap, ff), F32),
            pltpu.SemaphoreType.DMA((len(small),)),
            pltpu.SemaphoreType.DMA((3,)),
            pltpu.SemaphoreType.DMA((7,)),
            pltpu.SemaphoreType.DMA((7,)),
            pltpu.SemaphoreType.DMA((2, 2 * len(counts))),
            pltpu.SemaphoreType.DMA((2, splits, nh - 1)),
            *[
                shape
                for count in counts
                for shape in (
                    pltpu.VMEM((nb, cap * count, LANES), BF16),
                    pltpu.VMEM((n, cap * count, LANES), BF16),
                    pltpu.VMEM((n, cap * count, LANES), BF16),
                    pltpu.VMEM((n, cap * count, LANES), BF16),
                    pltpu.VMEM((n * cap, count * LANES), BF16),
                )
            ],
        ],
        compiler_params=pltpu.CompilerParams(
            collective_id=0, has_side_effects=True, vmem_limit_bytes=60 * 1024 * 1024
        ),
        name="layer",
    )(*small, out_weight, expert_up, expert_down).astype(BF16)


def solution(mesh):
    tokens = P(("head", "blk"), None)
    in_specs = (
        tokens, tokens, tokens, tokens,
        P("head", None), P(), P(), P(), P(),
        P("blk", None, "head"), P("blk", "head", None), tokens, tokens,
    )
    return jax.shard_map(
        functools.partial(on_device, mesh.shape["head"], mesh.shape["blk"]),
        mesh=mesh, in_specs=in_specs, out_specs=tokens, check_vma=False,
    )
```
